256 devices in a mesh: sector: 16 (over y_lo, z), ax: 4 (over y_hi, core), rad: 4 (over x).
Axes of the slice: x: 4, y: 4 (y_hi: 2, y_lo: 2; y = y_hi * 2 + y_lo), z: 8, core: 2. Of those that a mesh axis runs over, the one named last changes fastest.
Arguments:
- mass_excess: float32 [256, 128, 512], P('sector', 'ax', 'rad'), may hold values from -0.3 to 0.3
- speed_vector: float32 [3, 256, 128, 512], P(None, 'sector', 'ax', 'rad'), may hold values from -3 to 3
- thermal_excess: float32 [256, 128, 512], P('sector', 'ax', 'rad'), may hold values from -0.5 to 0.5
- energy_release: float32 [256, 128, 512], P('sector', 'ax', 'rad'), may hold values from -8 to 8
Outputs:
- new_density: float32 [256, 128, 512], P('sector', 'ax', 'rad')
- new_velocity: float32 [3, 256, 128, 512], P(None, 'sector', 'ax', 'rad')
- new_temperature: float32 [256, 128, 512], P('sector', 'ax', 'rad')
- harmonics: float32 [128, 128, 512], P('sector', 'ax', 'rad')
The draws below stay inside these ranges and needn't reach their ends.
All inputs are finite; a program needn't handle non-finite values.
Results may differ from the reference program's by a relative error of at most 0.00007.
Values sent between devices are 32-bit elements; how exact they have to be, the bound alone decides.
No kernel may reach another device: no remote copies, remote signals or barrier semaphores. Data moves between devices by JAX's collectives and lax.ppermute only.
A program may use at most 64 MiB of HBM per device.

```python
import math
import jax
import jax.numpy as jnp
from jax import lax

HARM = 128
ROUND_COUNT = 256
LENGTHWISE_COUNT = 128
OUTWARD_COUNT = 512


def level_of(key, dims, pieces, least, top_value):
    factor_of, own = 1.0, jax.random.fold_in(key, 6)
    for axis_at, blocks in pieces:
        steps = jnp.exp(jax.random.uniform(jax.random.fold_in(own, axis_at), (blocks,), jnp.float32, least / len(pieces), top_value / len(pieces)))
        factor_of = factor_of * jnp.repeat(steps, dims[axis_at] // blocks).reshape([-1 if axis == axis_at else 1 for axis in range(len(dims))])
    return factor_of


def scatter_about(key, dims, deviation, reach, split=(), held_as=jnp.bfloat16):
    result = jax.random.normal(key, dims, jnp.float32) * deviation
    if len(split) > 0:
        result = level_of(key, dims, split, -0.22, 0.18) * result
    return jnp.clip(result, min=-reach, max=reach).astype(held_as)


def setup_inputs(seed: int = 0) -> dict:
    key_list = jax.random.split(jax.random.key(seed), 5)
    mass_excess = jnp.clip(jax.random.uniform(key_list[0], (ROUND_COUNT, LENGTHWISE_COUNT, OUTWARD_COUNT), jnp.float32, -0.3, 0.3) * level_of(key_list[0], (ROUND_COUNT, LENGTHWISE_COUNT, OUTWARD_COUNT), ((0, 16), (1, 4), (2, 4)), -0.4, 0.0), -0.3, 0.3)
    speed_vector = scatter_about(key_list[1], (3, ROUND_COUNT, LENGTHWISE_COUNT, OUTWARD_COUNT), 0.5, 3.0, ((1, 16), (2, 4), (3, 4)), jnp.float32)
    thermal_excess = jnp.clip(jax.random.uniform(key_list[2], (ROUND_COUNT, LENGTHWISE_COUNT, OUTWARD_COUNT), jnp.float32, -0.5, 0.5) * level_of(key_list[2], (ROUND_COUNT, LENGTHWISE_COUNT, OUTWARD_COUNT), ((0, 16), (1, 4), (2, 4)), -0.4, 0.0), -0.5, 0.5)
    energy_release = scatter_about(key_list[3], (ROUND_COUNT, LENGTHWISE_COUNT, OUTWARD_COUNT), 2.0, 8.0, ((0, 16), (1, 4), (2, 4)), jnp.float32)
    return dict(mass_excess=mass_excess, speed_vector=speed_vector, thermal_excess=thermal_excess, energy_release=energy_release)


HEAT_RATIO = 1.4
STEP_DT = 0.1
VISCOSITY = 0.1
DIFFUSIVITY = 0.1

def first_diff(padded_fields, array_axis):
    length = padded_fields.shape[array_axis] - 4

    def take(offset):
        return lax.slice_in_dim(padded_fields, offset, offset + length, axis=array_axis)
    return (8.0 * (take(3) - take(1)) - (take(4) - take(0))) / 12.0

def second_diff(padded_fields, array_axis):
    length = padded_fields.shape[array_axis] - 4

    def take(offset):
        return lax.slice_in_dim(padded_fields, offset, offset + length, axis=array_axis)
    return (16.0 * (take(3) + take(1)) - 30.0 * take(2) - (take(4) + take(0))) / 12.0

def advance(fluid_snapshot, padded_list, energy_release, spacing_theta):
    mass_excess = fluid_snapshot[0]
    speed_vector = fluid_snapshot[1:4]
    thermal_profile = fluid_snapshot[4]
    inverse = 1.0 / (1.0 + mass_excess)
    continuity = jnp.zeros_like(mass_excess)
    convective_transport = jnp.zeros_like(fluid_snapshot[1:5])
    diffusion_operator = jnp.zeros_like(fluid_snapshot[1:5])
    spreading_sum = jnp.zeros_like(mass_excess)
    pressure_terms = []
    for direction in range(3):
        padded_fields = padded_list[direction]
        spacing = spacing_theta if direction == 0 else 1.0
        slopes = first_diff(padded_fields, direction + 1) / spacing
        curves = second_diff(padded_fields[1:5], direction + 1) / (spacing * spacing)
        mass_flux = (1.0 + padded_fields[0]) * padded_fields[1 + direction]
        pressure = (1.0 + padded_fields[0]) * (1.0 + padded_fields[4]) / HEAT_RATIO
        continuity = continuity - first_diff(mass_flux, direction) / spacing
        pressure_terms.append(first_diff(pressure, direction) / spacing)
        convective_transport = convective_transport + speed_vector[direction][None] * slopes[1:5]
        diffusion_operator = diffusion_operator + curves
        spreading_sum = spreading_sum + slopes[1 + direction]
    velocity_rate = -convective_transport[0:3] - jnp.stack(pressure_terms) * inverse[None] + VISCOSITY * diffusion_operator[0:3]
    warming_derivative = -convective_transport[3] - (HEAT_RATIO - 1.0) * (1.0 + thermal_profile) * spreading_sum + DIFFUSIVITY * diffusion_operator[3] + energy_release
    rates = jnp.concatenate([continuity[None], velocity_rate, warming_derivative[None]], axis=0)
    return fluid_snapshot + STEP_DT * rates

def harmonic_basis(rows, thetas, ntheta, harm):
    half = harm // 2
    orders = jnp.where(rows <= half, rows, rows - half).astype(jnp.int32)
    use_sine = rows > half
    phase = orders[:, None] * thetas[None, :].astype(jnp.int32) % ntheta
    angle = phase.astype(jnp.float32) * (2.0 * math.pi / ntheta)
    values = jnp.where(use_sine[:, None], jnp.sin(angle), jnp.cos(angle))
    return values / math.sqrt(ntheta)

def reference(mass_excess, speed_vector, thermal_excess, energy_release):
    fluid_snapshot = jnp.concatenate([mass_excess[None], speed_vector, thermal_excess[None]], axis=0)
    theta_pad = jnp.pad(fluid_snapshot, ((0, 0), (2, 2), (0, 0), (0, 0)), mode='wrap')
    plane = jnp.pad(fluid_snapshot, ((0, 0), (0, 0), (2, 2), (2, 2)))
    axial_pad = plane[:, :, :, 2:-2]
    radial_pad = plane[:, :, 2:-2, :]
    radial_index = jnp.arange(OUTWARD_COUNT).astype(jnp.float32)
    spacing_theta = (0.5 + (radial_index + 0.5) / OUTWARD_COUNT).reshape(1, 1, OUTWARD_COUNT)
    fresh = advance(fluid_snapshot, [theta_pad, axial_pad, radial_pad], energy_release, spacing_theta)
    new_temper = fresh[4]
    basis = harmonic_basis(jnp.arange(HARM).astype(jnp.int32), jnp.arange(ROUND_COUNT).astype(jnp.int32), ROUND_COUNT, HARM)
    coeffs = jnp.dot(basis, new_temper.reshape(ROUND_COUNT, LENGTHWISE_COUNT * OUTWARD_COUNT), precision=lax.Precision.HIGHEST, preferred_element_type=jnp.float32)
    return (fresh[0], fresh[1:4], new_temper, coeffs.reshape(HARM, LENGTHWISE_COUNT, OUTWARD_COUNT))
```

```python
import math

import jax
import jax.numpy as jnp
import numpy as np
from jax import lax
from jax.experimental import pallas as pl
from jax.experimental.pallas import tpu as pltpu
from jax.sharding import PartitionSpec as P

HARM = 128
HEAT_RATIO = 1.4
STEP_DT = 0.1
VISCOSITY = 0.1
DIFFUSIVITY = 0.1
VMEM_LIMIT = 40 * 1024 * 1024


def basis_table(ntheta):
    half = HARM // 2
    rows = np.arange(HARM)
    orders = np.where(rows <= half, rows, rows - half)
    phase = orders[:, None] * np.arange(ntheta)[None, :] % ntheta
    angle = phase * (2.0 * math.pi / ntheta)
    values = np.where((rows > half)[:, None], np.sin(angle), np.cos(angle))
    return (values / math.sqrt(ntheta)).astype(np.float32)


def edges_kernel(rho, vel, temp, s_lo, s_hi, a_lo, a_hi, r_pack):
    nt, na, nr = rho.shape
    fields = [rho, vel.at[0], vel.at[1], vel.at[2], temp]
    lane = lax.broadcasted_iota(jnp.int32, (na, nr), 1)
    for f, ref in enumerate(fields):
        s_lo[f] = ref[0:2]
        s_hi[f] = ref[nt - 2 : nt]
        packed = jnp.zeros((na, nr), jnp.float32)
        for t in range(nt):
            for side in range(2):
                a_lo[f, side, pl.ds(t, 1), :] = ref[t, pl.ds(side, 1), :]
                a_hi[f, side, pl.ds(t, 1), :] = ref[t, pl.ds(na - 2 + side, 1), :]
            x = ref[t]
            turned = pltpu.roll(x, 8 * t, 1) if t else x
            near = (lane + 2 - 8 * t) % nr < 4
            packed = jnp.where(near, turned, packed)
        r_pack[f] = packed


def stencil_kernel(
    rho, vel, temp, heat, s_lo, s_hi, a_lo, a_hi, r_left, r_right,
    new_rho, new_vel, new_temp, cells,
    pad, flux_t, flux_a, flux_r, press, r_halo,
):
    nt, na, nr = rho.shape
    ax, rad = lax.axis_index("ax"), lax.axis_index("rad")
    nax, nrad = lax.axis_size("ax"), lax.axis_size("rad")
    keep_al = jnp.where(ax > 0, 1.0, 0.0)
    keep_ah = jnp.where(ax < nax - 1, 1.0, 0.0)
    keep_rl = jnp.where(rad > 0, 1.0, 0.0)
    keep_rh = jnp.where(rad < nrad - 1, 1.0, 0.0)
    fields = [rho, vel.at[0], vel.at[1], vel.at[2], temp]
    lane = lax.broadcasted_iota(jnp.int32, (na, nr), 1)
    mod8 = lane % 8
    for f, ref in enumerate(fields):
        pad[f, 0:2, 8 : 8 + na] = s_lo[f]
        pad[f, nt + 2 : nt + 4, 8 : 8 + na] = s_hi[f]
        for t in range(nt):
            pad[f, t + 2, 8 : 8 + na] = ref[t]
            for side in range(2):
                pad[f, t + 2, 6 + side : 7 + side] = a_lo[f, side, pl.ds(t, 1), :] * keep_al
                pad[f, t + 2, 8 + na + side : 9 + na + side] = (
                    a_hi[f, side, pl.ds(t, 1), :] * keep_ah
                )
        r_halo[f] = jnp.where(mod8 < 2, r_right[f] * keep_rh, r_left[f] * keep_rl)
    r_halo[5] = (1.0 + r_halo[0]) * r_halo[3]
    r_halo[6] = (1.0 + r_halo[0]) * (1.0 + r_halo[4])

    def products(t, carry):
        mass = 1.0 + pad[0, t]
        flux_t[t] = mass * pad[1, t]
        press[t] = mass * (1.0 + pad[4, t])
        return carry

    lax.fori_loop(0, nt + 4, products, 0)

    def products_in(t, carry):
        mass = 1.0 + pad[0, t + 2]
        flux_a[t] = mass * pad[2, t + 2]
        flux_r[t] = mass[8 : 8 + na] * pad[3, t + 2, 8 : 8 + na]
        return carry

    lax.fori_loop(0, nt, products_in, 0)

    sub = 8
    lane8 = lax.broadcasted_iota(jnp.int32, (sub, nr), 1)
    radius = (rad * nr + lane8).astype(jnp.float32)
    h = 0.5 + (radius + 0.5) / (nr * nrad)
    inv12h = 1.0 / (12.0 * h)
    inv12 = 1.0 / 12.0
    gt = VISCOSITY / (12.0 * h * h)
    g = VISCOSITY / 12.0
    first, last = lane8 == 0, lane8 == nr - 1
    first2, last2 = lane8 < 2, lane8 >= nr - 2

    def step(t, carry):
        turn = (nr - 8 * t) % nr
        halos = [pltpu.roll(r_halo[q], turn, 1) for q in range(1, 7)]
        for j in range(na // sub):
            lo = 8 + j * sub
            rows = slice(lo, lo + sub)

            def lanes(mid, halo):
                ht = halo[j * sub : (j + 1) * sub]
                return [
                    pltpu.roll(jnp.where(last2, ht, mid), 2, 1),
                    pltpu.roll(jnp.where(last, ht, mid), 1, 1),
                    pltpu.roll(jnp.where(first, ht, mid), nr - 1, 1),
                    pltpu.roll(jnp.where(first2, ht, mid), nr - 2, 1),
                ]

            def around(ref, mid, halo):
                return (
                    [ref[t + 2 + d, rows] for d in (-2, -1, 1, 2)],
                    [ref[t + 2, lo + d : lo + d + sub] for d in (-2, -1, 1, 2)],
                    lanes(mid, halo),
                )

            def d1(s):
                return 8.0 * (s[2] - s[1]) - (s[3] - s[0])

            r0 = pad[0, t + 2, rows]
            u = [pad[1 + c, t + 2, rows] for c in range(3)]
            w = [u[0] * inv12h, u[1] * inv12, u[2] * inv12]
            fresh = []
            div = None
            for c in range(1, 5):
                mid = u[c - 1] if c < 4 else pad[4, t + 2, rows]
                st, sa, sr = around(pad.at[c], mid, halos[c - 1])
                slopes = [d1(st), d1(sa), d1(sr)]
                if c < 4:
                    part = slopes[c - 1] * (inv12h if c == 1 else inv12)
                    div = part if div is None else div + part
                ring1 = (sa[1] + sa[2]) + (sr[1] + sr[2])
                ring2 = (sa[0] + sa[3]) + (sr[0] + sr[3])
                curve_t = 16.0 * (st[1] + st[2]) - 30.0 * mid - (st[0] + st[3])
                curve = 16.0 * ring1 - 60.0 * mid - ring2
                rate = gt * curve_t + g * curve - (
                    w[0] * slopes[0] + w[1] * slopes[1] + w[2] * slopes[2]
                )
                fresh.append((mid, rate))
            mid, rate = fresh[3]
            rate = rate - (HEAT_RATIO - 1.0) * (1.0 + mid) * div + heat[t, j * sub : (j + 1) * sub]
            value = mid + STEP_DT * rate
            new_temp[t, j * sub : (j + 1) * sub] = value

            pmid = press[t + 2, rows]
            pt, pa, pr = around(press, pmid, halos[5])
            scale = 1.0 / (HEAT_RATIO * (1.0 + r0))
            grads = [d1(pt) * inv12h, d1(pa) * inv12, d1(pr) * inv12]
            for c in range(3):
                mid, rate = fresh[c]
                new_vel[c, t, j * sub : (j + 1) * sub] = mid + STEP_DT * (rate - grads[c] * scale)

            ft = [flux_t[t + 2 + d, rows] for d in (-2, -1, 1, 2)]
            fa = [flux_a[t, lo + d : lo + d + sub] for d in (-2, -1, 1, 2)]
            fr = lanes(flux_r[t, j * sub : (j + 1) * sub], halos[4])
            loss = d1(ft) * inv12h + (d1(fa) + d1(fr)) * inv12
            new_rho[t, j * sub : (j + 1) * sub] = r0 - STEP_DT * loss
        return carry

    lax.fori_loop(0, nt, step, 0)
    flat = new_temp.reshape(nt * na, nr)
    for a in range(na):
        cells[a] = flat[pl.ds(a, nt, stride=na), :]


def harmonics_kernel(table, spread, out):
    sectors, parts, nt, nr = spread.shape
    for p in range(parts):
        x = spread[:, p].reshape(sectors * nt, nr)
        y = jnp.dot(
            table[...], x, precision=lax.Precision.HIGHEST, preferred_element_type=jnp.float32
        )
        out[:, p] = y.reshape(sectors, HARM // sectors, nr)


def gather_kernel(parts, out):
    cells, rows, nr = parts.shape
    flat = parts.reshape(cells * rows, nr)
    for k in range(rows):
        out[k] = flat[pl.ds(k, cells, stride=rows), :]


def per_device(table, mass_excess, speed_vector, thermal_excess, energy_release):
    nt, na, nr = mass_excess.shape
    f32 = jnp.float32
    params = pltpu.CompilerParams(vmem_limit_bytes=VMEM_LIMIT)
    sds = jax.ShapeDtypeStruct
    s_lo, s_hi, a_lo, a_hi, r_pack = pl.pallas_call(
        edges_kernel,
        out_shape=(
            sds((5, 2, na, nr), f32),
            sds((5, 2, na, nr), f32),
            sds((5, 2, nt, nr), f32),
            sds((5, 2, nt, nr), f32),
            sds((5, na, nr), f32),
        ),
        compiler_params=params,
        name="edges",
    )(mass_excess, speed_vector, thermal_excess)

    def ring(axis, up):
        count = lax.axis_size(axis)
        return [(i, (i + (1 if up else -1)) % count) for i in range(count)]

    t_lo = lax.ppermute(s_hi, "sector", ring("sector", True))
    t_hi = lax.ppermute(s_lo, "sector", ring("sector", False))
    x_lo = lax.ppermute(a_hi, "ax", ring("ax", True))
    x_hi = lax.ppermute(a_lo, "ax", ring("ax", False))
    r_left = lax.ppermute(r_pack, "rad", ring("rad", True))
    r_right = lax.ppermute(r_pack, "rad", ring("rad", False))
    new_rho, new_vel, new_temp, cells = pl.pallas_call(
        stencil_kernel,
        out_shape=(
            sds((nt, na, nr), f32),
            sds((3, nt, na, nr), f32),
            sds((nt, na, nr), f32),
            sds((na, nt, nr), f32),
        ),
        scratch_shapes=[
            pltpu.VMEM((5, nt + 4, na + 16, nr), f32),
            pltpu.VMEM((nt + 4, na + 16, nr), f32),
            pltpu.VMEM((nt, na + 16, nr), f32),
            pltpu.VMEM((nt, na, nr), f32),
            pltpu.VMEM((nt + 4, na + 16, nr), f32),
            pltpu.VMEM((7, na, nr), f32),
        ],
        compiler_params=params,
        name="stencil",
    )(
        mass_excess, speed_vector, thermal_excess, energy_release,
        t_lo, t_hi, x_lo, x_hi, r_left, r_right,
    )
    sectors = lax.axis_size("sector")
    rows = HARM // sectors
    share = na // sectors
    spread = lax.all_to_all(
        cells.reshape(sectors, share, nt, nr), "sector", 0, 0, tiled=True
    )
    terms = pl.pallas_call(
        harmonics_kernel,
        out_shape=sds((sectors, share, rows, nr), f32),
        compiler_params=params,
        name="harmonics",
    )(table, spread)
    terms = lax.all_to_all(terms, "sector", 0, 0, tiled=True)
    coeffs = pl.pallas_call(
        gather_kernel,
        out_shape=sds((rows, na, nr), f32),
        compiler_params=params,
        name="gather",
    )(terms.reshape(na, rows, nr))
    return (new_rho, new_vel, new_temp, coeffs)


def solution(mesh):
    cell = P("sector", "ax", "rad")
    vector = P(None, "sector", "ax", "rad")

    def run(mass_excess, speed_vector, thermal_excess, energy_release):
        table = jnp.asarray(basis_table(mass_excess.shape[0]))
        return jax.shard_map(
            per_device,
            mesh=mesh,
            in_specs=(P(), cell, vector, cell, cell),
            out_specs=(cell, vector, cell, cell),
            check_vma=False,
        )(table, mass_excess, speed_vector, thermal_excess, energy_release)

    return run
```

```python
import math

import jax
import jax.numpy as jnp
import numpy as np
from jax import lax
from jax.experimental import pallas as pl
from jax.experimental.pallas import tpu as pltpu
from jax.sharding import PartitionSpec as P

HARM = 128
HEAT_RATIO = 1.4
STEP_DT = 0.1
VISCOSITY = 0.1
DIFFUSIVITY = 0.1
VMEM_LIMIT = 16 * 1024 * 1024


def basis_table(ntheta):
    half = HARM // 2
    rows = np.arange(HARM)
    orders = np.where(rows <= half, rows, rows - half)
    phase = orders[:, None] * np.arange(ntheta)[None, :] % ntheta
    angle = phase * (2.0 * math.pi / ntheta)
    values = np.where((rows > half)[:, None], np.sin(angle), np.cos(angle))
    return (values / math.sqrt(ntheta)).astype(np.float32)


def edge_rows(ref, f, first, count, stride):
    lead, rows, lanes = ref.shape[1:]
    return ref.at[f].reshape(lead * rows, lanes).at[pl.ds(first, count, stride=stride), :]


def edges_kernel(rho, vel, temp, s_lo, s_hi, a_lo, a_hi, r_pack, held, sems):
    nt, na, nr = rho.shape
    sources = [rho, vel.at[0], vel.at[1], vel.at[2], temp]
    copies = [
        pltpu.make_async_copy(src, held.at[f], sems.at[f]) for f, src in enumerate(sources)
    ]
    for copy in copies:
        copy.start()
    lane = lax.broadcasted_iota(jnp.int32, (na, nr), 1)
    for f, copy in enumerate(copies):
        copy.wait()
        s_lo[f] = held[f, 0:2]
        s_hi[f] = held[f, nt - 2 : nt]
        for side in range(2):
            a_lo[f, side] = edge_rows(held, f, side, nt, na)[...]
            a_hi[f, side] = edge_rows(held, f, na - 2 + side, nt, na)[...]
        shift = 4 * (f % 2)
        packed = r_pack[f // 2] if f % 2 else jnp.zeros((na, nr), jnp.float32)
        for t in range(nt):
            turn = (8 * t + shift) % nr
            x = held[f, t]
            turned = pltpu.roll(x, turn, 1) if turn else x
            near = (lane + 2 - turn) % nr < 4
            packed = jnp.where(near, turned, packed)
        r_pack[f // 2] = packed


def place():
    ax, rad = lax.axis_index("ax"), lax.axis_index("rad")
    nax, nrad = lax.axis_size("ax"), lax.axis_size("rad")
    keep = [
        jnp.where(c, 1.0, 0.0) for c in (ax > 0, ax < nax - 1, rad > 0, rad < nrad - 1)
    ]
    return keep, rad, nrad


def fill(pad, halos, r_halo, keep):
    s_lo, s_hi, a_lo, a_hi, r_left, r_right = halos
    nt, na, nr = pad.shape[1] - 4, pad.shape[2] - 16, pad.shape[3]
    rows = na + 16
    for f in range(5):
        pad[f, 0:2, 8 : 8 + na] = s_lo[f]
        pad[f, nt + 2 : nt + 4, 8 : 8 + na] = s_hi[f]
    for f in range(5):
        for side in range(2):
            edge_rows(pad, f, 2 * rows + 6 + side, nt, rows)[...] = a_lo[f, side] * keep[0]
            edge_rows(pad, f, 2 * rows + 8 + na + side, nt, rows)[...] = a_hi[f, side] * keep[1]
    join_packs(r_halo, r_left, r_right, keep)


def join_packs(r_halo, r_left, r_right, keep):
    mod4 = lax.broadcasted_iota(jnp.int32, r_left.shape[1:], 1) % 4
    for q in range(r_left.shape[0]):
        r_halo[q] = jnp.where(mod4 < 2, r_right[q] * keep[3], r_left[q] * keep[2])


def spacings(rad, nrad, nr):
    lane = lax.broadcasted_iota(jnp.int32, (8, nr), 1)
    radius = (rad * nr + lane).astype(jnp.float32)
    h = 0.5 + (radius + 0.5) / (nr * nrad)
    return 1.0 / (12.0 * h), VISCOSITY / (12.0 * h * h), lane


def d1(s):
    return 8.0 * (s[2] - s[1]) - (s[3] - s[0])


def lane_shifts(mid, halo, lane):
    nr = mid.shape[-1]
    return [
        pltpu.roll(jnp.where(lane >= nr - 2, halo, mid), 2, 1),
        pltpu.roll(jnp.where(lane == nr - 1, halo, mid), 1, 1),
        pltpu.roll(jnp.where(lane == 0, halo, mid), nr - 1, 1),
        pltpu.roll(jnp.where(lane < 2, halo, mid), nr - 2, 1),
    ]


def t_shifts(ref, t, lo):
    return [ref[t + 2 + d, lo : lo + 8] for d in (-2, -1, 1, 2)]


def a_shifts(ref, t, lo):
    return [ref[t + 2, lo + d : lo + d + 8] for d in (-2, -1, 1, 2)]


def transport(mid, st, sa, sr, w, gt):
    ring1 = (sa[1] + sa[2]) + (sr[1] + sr[2])
    ring2 = (sa[0] + sa[3]) + (sr[0] + sr[3])
    curve_t = 16.0 * (st[1] + st[2]) - 30.0 * mid - (st[0] + st[3])
    curve = 16.0 * ring1 - 60.0 * mid - ring2
    return gt * curve_t + (VISCOSITY / 12.0) * curve - (
        w[0] * d1(st) + w[1] * d1(sa) + w[2] * d1(sr)
    )


def inner_kernel(vel, temp, heat, base, pad):
    nt, na, nr = heat.shape
    rad, nrad = lax.axis_index("rad"), lax.axis_size("rad")
    zeros = jnp.zeros((2, na, nr), jnp.float32)
    for q, ref in enumerate((vel.at[0], vel.at[1], temp)):
        pad[q, 2 : nt + 2, 8 : 8 + na] = ref[...]
        pad[q, 0:2, 8 : 8 + na] = zeros
        pad[q, nt + 2 : nt + 4, 8 : 8 + na] = zeros
        for t in range(nt):
            pad[q, t + 2, 0:8] = zeros[0, 0:8]
            pad[q, t + 2, 8 + na : 16 + na] = zeros[0, 0:8]
    inv12h, gt, lane = spacings(rad, nrad, nr)
    inv12 = 1.0 / 12.0

    def step(t, carry):
        for j in range(na // 8):
            lo, out = 8 + j * 8, slice(j * 8, j * 8 + 8)
            u = [vel[c, t, out] for c in range(3)]
            w = [u[0] * inv12h, u[1] * inv12, u[2] * inv12]
            div = (
                d1(t_shifts(pad.at[0], t, lo)) * inv12h
                + (d1(a_shifts(pad.at[1], t, lo)) + d1(lane_shifts(u[2], 0.0, lane))) * inv12
            )
            mid = temp[t, out]
            rate = transport(
                mid,
                t_shifts(pad.at[2], t, lo),
                a_shifts(pad.at[2], t, lo),
                lane_shifts(mid, 0.0, lane),
                w,
                gt,
            )
            rate = rate - (HEAT_RATIO - 1.0) * (1.0 + mid) * div + heat[t, out]
            base[t, out] = mid + STEP_DT * rate
        return carry

    lax.fori_loop(0, nt, step, 0, unroll=2)


def low_parts(n, place):
    if place == 0:
        return n[0] - 8.0 * n[1], 16.0 * n[1] - n[0]
    return n[1], -n[1]


def high_parts(p, place):
    if place == 0:
        return 8.0 * p[0] - p[1], 16.0 * p[0] - p[1]
    return -p[0], -p[0]


def halo_share(mid, u, c, g, t_parts, u_parts):
    slope, curve = t_parts
    return STEP_DT * (
        g * curve - c * (u * slope + (HEAT_RATIO - 1.0) * (1.0 + mid) * u_parts[0])
    )


def pack_parts(x):
    nr = x.shape[-1]
    mod4 = lax.broadcasted_iota(jnp.int32, x.shape, 1) % 4
    up1, up2 = pltpu.roll(x, nr - 1, 1), pltpu.roll(x, nr - 2, 1)
    down1, down2 = pltpu.roll(x, 1, 1), pltpu.roll(x, 2, 1)
    above, inner, outer = mod4 >= 2, mod4 == 3, mod4 == 0
    slope = jnp.where(
        above,
        jnp.where(inner, 8.0 * up1, 0.0) - up2,
        down2 - jnp.where(outer, 8.0 * down1, 0.0),
    )
    curve = jnp.where(
        above,
        jnp.where(inner, 16.0 * up1, 0.0) - up2,
        jnp.where(outer, 16.0 * down1, 0.0) - down2,
    )
    return slope, curve


def temperature_kernel(
    vel, temp, base, s_lo, s_hi, a_lo, a_hi, r_left, r_right, cells, r_halo
):
    nt, na, nr = base.shape
    keep, rad, nrad = place()
    join_packs(r_halo, r_left, r_right, keep)
    inv12h, gt, lane = spacings(rad, nrad, nr)
    inv12, g = 1.0 / 12.0, VISCOSITY / 12.0
    turned = cells.reshape(na * nt, nr)
    edge = (lane < 2) | (lane >= nr - 2)
    u_slope, _ = pack_parts(r_halo[1])
    t_slope, t_curve = pack_parts(r_halo[2])
    for t in range(nt):
        even, odd = (nr - 8 * t) % nr, (2 * nr - 8 * t - 4) % nr
        ts = pltpu.roll(t_slope, even, 1) if even else t_slope
        tc = pltpu.roll(t_curve, even, 1) if even else t_curve
        us = pltpu.roll(u_slope, odd, 1) if odd else u_slope
        for j in range(na // 8):
            out = slice(j * 8, j * 8 + 8)
            mid = temp[t, out]
            share = halo_share(mid, vel[2, t, out], inv12, g, (ts[out], tc[out]), (us[out],))
            value = base[t, out] + jnp.where(edge, share, 0.0)
            parts = None
            if t < 2:
                parts = [low_parts((s_lo[f, 0, out], s_lo[f, 1, out]), t) for f in (4, 1)]
            elif t >= nt - 2:
                parts = [
                    high_parts((s_hi[f, 0, out], s_hi[f, 1, out]), nt - 1 - t) for f in (4, 1)
                ]
            if parts is not None:
                value = value + halo_share(mid, vel[0, t, out], inv12h, gt, *parts)
            turned[pl.ds(j * 8 * nt + t, 8, stride=nt), :] = value
    rows, speeds = temp.reshape(nt * na, nr), vel.at[1].reshape(nt * na, nr)
    for a in (0, 1, na - 2, na - 1):
        mid, u = rows[pl.ds(a, nt, stride=na), :], speeds[pl.ds(a, nt, stride=na), :]
        if a < 2:
            parts = [low_parts((a_lo[f, 0], a_lo[f, 1]), a) for f in (4, 2)]
            scale = keep[0]
        else:
            parts = [high_parts((a_hi[f, 0], a_hi[f, 1]), na - 1 - a) for f in (4, 2)]
            scale = keep[1]
        cells[a] = cells[a] + scale * halo_share(mid, u, inv12, g, *parts)


def flow_kernel(
    rho, vel, temp, cells, s_lo, s_hi, a_lo, a_hi, r_left, r_right,
    new_rho, new_vel, new_temp,
    full, flux_t, flux_a, flux_r, press, r_halo,
):
    nt, na, nr = new_rho.shape
    keep, rad, nrad = place()
    for f, ref in enumerate((rho, vel.at[0], vel.at[1], vel.at[2], temp)):
        full[f, 2 : nt + 2, 8 : 8 + na] = ref[...]
    halos = (s_lo, s_hi, a_lo, a_hi, r_left, r_right)
    fill(full, halos, r_halo, keep)

    def products(t, carry):
        mass = 1.0 + full[0, t]
        flux_t[t] = mass * full[1, t]
        press[t] = mass * (1.0 + full[4, t])
        return carry

    lax.fori_loop(0, nt + 4, products, 0)

    def products_in(t, carry):
        mass = 1.0 + full[0, t + 2]
        flux_a[t + 2] = mass * full[2, t + 2]
        flux_r[t] = mass[8 : 8 + na] * full[3, t + 2, 8 : 8 + na]
        return carry

    lax.fori_loop(0, nt, products_in, 0)
    inv12h, gt, lane = spacings(rad, nrad, nr)
    inv12 = 1.0 / 12.0
    turned = cells.reshape(na * nt, nr)

    def step(t, carry):
        even, odd = (nr - 8 * t) % nr, (2 * nr - 8 * t - 4) % nr
        hr, h0, h1, h2, ht = [
            pltpu.roll(r_halo[f // 2], odd if f % 2 else even, 1) for f in range(5)
        ]
        turned_halo = [h0, h1, h2, (1.0 + hr) * h2, (1.0 + hr) * (1.0 + ht)]
        for j in range(na // 8):
            lo, out = 8 + j * 8, slice(j * 8, j * 8 + 8)
            halo = [x[out] for x in turned_halo]
            r0 = full[0, t + 2, lo : lo + 8]
            u = [full[1 + c, t + 2, lo : lo + 8] for c in range(3)]
            w = [u[0] * inv12h, u[1] * inv12, u[2] * inv12]
            scale = 1.0 / (HEAT_RATIO * (1.0 + r0))
            grads = [
                d1(t_shifts(press, t, lo)) * inv12h,
                d1(a_shifts(press, t, lo)) * inv12,
                d1(lane_shifts(press[t + 2, lo : lo + 8], halo[4], lane)) * inv12,
            ]
            for c in range(3):
                ref = full.at[1 + c]
                rate = transport(
                    u[c],
                    t_shifts(ref, t, lo),
                    a_shifts(ref, t, lo),
                    lane_shifts(u[c], halo[c], lane),
                    w,
                    gt,
                )
                new_vel[c, t, out] = u[c] + STEP_DT * (rate - grads[c] * scale)
            loss = (
                d1(t_shifts(flux_t, t, lo)) * inv12h
                + (
                    d1(a_shifts(flux_a, t, lo))
                    + d1(lane_shifts(flux_r[t, out], halo[3], lane))
                )
                * inv12
            )
            new_rho[t, out] = r0 - STEP_DT * loss
            new_temp[t, out] = turned[pl.ds(j * 8 * nt + t, 8, stride=nt), :]
        return carry

    lax.fori_loop(0, nt, step, 0)


def harmonics_kernel(table, spread, out, held, sems):
    sectors, parts, nt, nr = spread.shape
    copies = []
    for p in range(parts):
        x = spread[:, p].reshape(sectors * nt, nr)
        y = jnp.dot(
            table[...], x, precision=lax.Precision.HIGHEST, preferred_element_type=jnp.float32
        )
        held[p] = y.reshape(sectors, HARM // sectors, nr)
        copies.append(pltpu.make_async_copy(held.at[p], out.at[:, p], sems.at[p]))
        copies[p].start()
    for copy in copies:
        copy.wait()


def gather_kernel(parts, out):
    cells, rows, nr = parts.shape
    flat = parts.reshape(cells * rows, nr)
    for k in range(rows):
        out[k] = flat[pl.ds(k, cells, stride=rows), :]


def per_device(table, mass_excess, speed_vector, thermal_excess, energy_release):
    nt, na, nr = mass_excess.shape
    f32 = jnp.float32
    params = pltpu.CompilerParams(vmem_limit_bytes=VMEM_LIMIT)
    sds = jax.ShapeDtypeStruct
    hbm = pl.BlockSpec(memory_space=pltpu.HBM)
    vmem = pl.BlockSpec(memory_space=pltpu.VMEM)
    padded = (nt + 4, na + 16, nr)
    s_lo, s_hi, a_lo, a_hi, r_pack = pl.pallas_call(
        edges_kernel,
        in_specs=[hbm] * 3,
        out_specs=[vmem] * 5,
        out_shape=(
            sds((5, 2, na, nr), f32),
            sds((5, 2, na, nr), f32),
            sds((5, 2, nt, nr), f32),
            sds((5, 2, nt, nr), f32),
            sds((3, na, nr), f32),
        ),
        scratch_shapes=[pltpu.VMEM((5, nt, na, nr), f32), pltpu.SemaphoreType.DMA((5,))],
        compiler_params=pltpu.CompilerParams(vmem_limit_bytes=54784 * 1024),
        name="edges",
    )(mass_excess, speed_vector, thermal_excess)

    def ring(axis, up):
        count = lax.axis_size(axis)
        return [(i, (i + (1 if up else -1)) % count) for i in range(count)]

    halos = (
        lax.ppermute(s_hi, "sector", ring("sector", True)),
        lax.ppermute(s_lo, "sector", ring("sector", False)),
        lax.ppermute(a_hi, "ax", ring("ax", True)),
        lax.ppermute(a_lo, "ax", ring("ax", False)),
        lax.ppermute(r_pack, "rad", ring("rad", True)),
        lax.ppermute(r_pack, "rad", ring("rad", False)),
    )
    (base,) = pl.pallas_call(
        inner_kernel,
        in_specs=[vmem] * 3,
        out_specs=[vmem],
        out_shape=(sds((nt, na, nr), f32),),
        scratch_shapes=[pltpu.VMEM((3, *padded), f32)],
        cost_estimate=pl.CostEstimate(
            flops=80 * nt * na * nr, bytes_accessed=24 * nt * na * nr, transcendentals=0
        ),
        compiler_params=params,
        name="inner",
    )(speed_vector, thermal_excess, energy_release)
    (cells,) = pl.pallas_call(
        temperature_kernel,
        in_specs=[vmem] * 9,
        out_specs=[vmem],
        out_shape=(sds((na, nt, nr), f32),),
        scratch_shapes=[pltpu.VMEM((3, na, nr), f32)],
        compiler_params=params,
        name="temperature",
    )(speed_vector, thermal_excess, base, *halos)
    sectors = lax.axis_size("sector")
    rows = HARM // sectors
    share = na // sectors
    spread = lax.all_to_all(
        cells.reshape(sectors, share, nt, nr), "sector", 0, 0, tiled=True
    )
    new_rho, new_vel, new_temp = pl.pallas_call(
        flow_kernel,
        in_specs=[vmem] * 10,
        out_shape=(
            sds((nt, na, nr), f32),
            sds((3, nt, na, nr), f32),
            sds((nt, na, nr), f32),
        ),
        scratch_shapes=[
            pltpu.VMEM((5, *padded), f32),
            pltpu.VMEM(padded, f32),
            pltpu.VMEM(padded, f32),
            pltpu.VMEM((nt, na, nr), f32),
            pltpu.VMEM(padded, f32),
            pltpu.VMEM((3, na, nr), f32),
        ],
        cost_estimate=pl.CostEstimate(
            flops=180 * nt * na * nr, bytes_accessed=44 * nt * na * nr, transcendentals=0
        ),
        compiler_params=params,
        name="flow",
    )(mass_excess, speed_vector, thermal_excess, cells, *halos)
    terms = pl.pallas_call(
        harmonics_kernel,
        in_specs=[vmem] * 2,
        out_specs=hbm,
        out_shape=sds((sectors, share, rows, nr), f32),
        scratch_shapes=[
            pltpu.VMEM((share, sectors, rows, nr), f32),
            pltpu.SemaphoreType.DMA((share,)),
        ],
        compiler_params=params,
        name="harmonics",
    )(table, spread)
    terms = lax.all_to_all(terms, "sector", 0, 0, tiled=True)
    coeffs = pl.pallas_call(
        gather_kernel,
        out_shape=sds((rows, na, nr), f32),
        compiler_params=params,
        name="gather",
    )(terms.reshape(na, rows, nr))
    return (new_rho, new_vel, new_temp, coeffs)


def solution(mesh):
    cell = P("sector", "ax", "rad")
    vector = P(None, "sector", "ax", "rad")

    def run(mass_excess, speed_vector, thermal_excess, energy_release):
        table = jnp.asarray(basis_table(mass_excess.shape[0]))
        return jax.shard_map(
            per_device,
            mesh=mesh,
            in_specs=(P(), cell, vector, cell, cell),
            out_specs=(cell, vector, cell, cell),
            check_vma=False,
        )(table, mass_excess, speed_vector, thermal_excess, energy_release)

    return run
```

```python
import math

import jax
import jax.numpy as jnp
import numpy as np
from jax import lax
from jax.experimental import pallas as pl
from jax.experimental.pallas import tpu as pltpu
from jax.sharding import PartitionSpec as P

HARM = 128
HEAT_RATIO = 1.4
STEP_DT = 0.1
VISCOSITY = 0.1
DIFFUSIVITY = 0.1
VMEM_LIMIT = 16 * 1024 * 1024
PACK_PLANES = 6


def basis_table(ntheta):
    half = HARM // 2
    rows = np.arange(HARM)
    orders = np.where(rows <= half, rows, rows - half)
    phase = orders[:, None] * np.arange(ntheta)[None, :] % ntheta
    angle = phase * (2.0 * math.pi / ntheta)
    values = np.where((rows > half)[:, None], np.sin(angle), np.cos(angle))
    return (values / math.sqrt(ntheta)).astype(np.float32)


def edge_rows(ref, f, first, count, stride):
    lead, rows, lanes = ref.shape[1:]
    return ref.at[f].reshape(lead * rows, lanes).at[pl.ds(first, count, stride=stride), :]


def sector_edges_kernel(rho, vel, temp, s_lo, s_hi, sems):
    nt = rho.shape[0]
    copies = []
    for f, src in enumerate((rho, vel.at[0], vel.at[1], vel.at[2], temp)):
        copies.append(pltpu.make_async_copy(src.at[0:2], s_lo.at[f], sems.at[2 * f]))
        copies.append(
            pltpu.make_async_copy(src.at[nt - 2 : nt], s_hi.at[f], sems.at[2 * f + 1])
        )
    for copy in copies:
        copy.start()
    for copy in copies:
        copy.wait()


def tile_edges_kernel(after, rho, vel, temp, a_lo, a_hi, r_pack):
    del after
    nt, na, nr = rho.shape
    sources = [rho, vel.at[0], vel.at[1], vel.at[2], temp]
    r_pack[3:] = jnp.zeros((r_pack.shape[0] - 3, na, nr), jnp.float32)
    lane = lax.broadcasted_iota(jnp.int32, (na, nr), 1)
    for f, held in enumerate(sources):
        flat = held.reshape(nt * na, nr)
        for side in range(2):
            a_lo[f, side] = flat[pl.ds(side, nt, stride=na), :]
            a_hi[f, side] = flat[pl.ds(na - 2 + side, nt, stride=na), :]
        shift = 4 * (f % 2)
        packed = r_pack[f // 2] if f % 2 else jnp.zeros((na, nr), jnp.float32)
        for t in range(nt):
            turn = (8 * t + shift) % nr
            x = held[t]
            turned = pltpu.roll(x, turn, 1) if turn else x
            near = (lane + 2 - turn) % nr < 4
            packed = jnp.where(near, turned, packed)
        r_pack[f // 2] = packed


def place():
    ax, rad = lax.axis_index("ax"), lax.axis_index("rad")
    nax, nrad = lax.axis_size("ax"), lax.axis_size("rad")
    keep = [
        jnp.where(c, 1.0, 0.0) for c in (ax > 0, ax < nax - 1, rad > 0, rad < nrad - 1)
    ]
    return keep, rad, nrad


def fill(pad, halos, r_halo, keep):
    s_lo, s_hi, a_lo, a_hi, r_left, r_right = halos
    nt, na, nr = pad.shape[1] - 4, pad.shape[2] - 16, pad.shape[3]
    rows = na + 16
    for f in range(5):
        pad[f, 0:2, 8 : 8 + na] = s_lo[f]
        pad[f, nt + 2 : nt + 4, 8 : 8 + na] = s_hi[f]
    for f in range(5):
        for side in range(2):
            edge_rows(pad, f, 2 * rows + 6 + side, nt, rows)[...] = a_lo[f, side] * keep[0]
            edge_rows(pad, f, 2 * rows + 8 + na + side, nt, rows)[...] = a_hi[f, side] * keep[1]
    join_packs(r_halo, r_left, r_right, keep)


def join_packs(r_halo, r_left, r_right, keep):
    mod4 = lax.broadcasted_iota(jnp.int32, r_left.shape[1:], 1) % 4
    for q in range(3):
        r_halo[q] = jnp.where(mod4 < 2, r_right[q] * keep[3], r_left[q] * keep[2])


def spacings(rad, nrad, nr):
    lane = lax.broadcasted_iota(jnp.int32, (8, nr), 1)
    radius = (rad * nr + lane).astype(jnp.float32)
    h = 0.5 + (radius + 0.5) / (nr * nrad)
    return 1.0 / (12.0 * h), VISCOSITY / (12.0 * h * h), lane


def d1(s):
    return 8.0 * (s[2] - s[1]) - (s[3] - s[0])


def lane_shifts(mid, halo, lane):
    nr = mid.shape[-1]
    return [
        pltpu.roll(jnp.where(lane >= nr - 2, halo, mid), 2, 1),
        pltpu.roll(jnp.where(lane == nr - 1, halo, mid), 1, 1),
        pltpu.roll(jnp.where(lane == 0, halo, mid), nr - 1, 1),
        pltpu.roll(jnp.where(lane < 2, halo, mid), nr - 2, 1),
    ]


def t_shifts(ref, t, lo):
    return [ref[t + 2 + d, lo : lo + 8] for d in (-2, -1, 1, 2)]


def a_shifts(ref, t, lo):
    return [ref[t + 2, lo + d : lo + d + 8] for d in (-2, -1, 1, 2)]


def transport(mid, st, sa, sr, w, gt):
    ring1 = (sa[1] + sa[2]) + (sr[1] + sr[2])
    ring2 = (sa[0] + sa[3]) + (sr[0] + sr[3])
    curve_t = 16.0 * (st[1] + st[2]) - 30.0 * mid - (st[0] + st[3])
    curve = 16.0 * ring1 - 60.0 * mid - ring2
    return gt * curve_t + (VISCOSITY / 12.0) * curve - (
        w[0] * d1(st) + w[1] * d1(sa) + w[2] * d1(sr)
    )


def inner_kernel(vel, temp, heat, base, pad):
    nt, na, nr = heat.shape
    rad, nrad = lax.axis_index("rad"), lax.axis_size("rad")
    zeros = jnp.zeros((2, na, nr), jnp.float32)
    for q, ref in enumerate((vel.at[0], vel.at[1], temp)):
        pad[q, 2 : nt + 2, 8 : 8 + na] = ref[...]
        pad[q, 0:2, 8 : 8 + na] = zeros
        pad[q, nt + 2 : nt + 4, 8 : 8 + na] = zeros
        for t in range(nt):
            pad[q, t + 2, 0:8] = zeros[0, 0:8]
            pad[q, t + 2, 8 + na : 16 + na] = zeros[0, 0:8]
    inv12h, gt, lane = spacings(rad, nrad, nr)
    inv12 = 1.0 / 12.0

    def step(t, carry):
        for j in range(na // 8):
            lo, out = 8 + j * 8, slice(j * 8, j * 8 + 8)
            u = [vel[c, t, out] for c in range(3)]
            w = [u[0] * inv12h, u[1] * inv12, u[2] * inv12]
            div = (
                d1(t_shifts(pad.at[0], t, lo)) * inv12h
                + (d1(a_shifts(pad.at[1], t, lo)) + d1(lane_shifts(u[2], 0.0, lane))) * inv12
            )
            mid = temp[t, out]
            rate = transport(
                mid,
                t_shifts(pad.at[2], t, lo),
                a_shifts(pad.at[2], t, lo),
                lane_shifts(mid, 0.0, lane),
                w,
                gt,
            )
            rate = rate - (HEAT_RATIO - 1.0) * (1.0 + mid) * div + heat[t, out]
            base[t, out] = mid + STEP_DT * rate
        return carry

    lax.fori_loop(0, nt, step, 0, unroll=2)


def low_parts(n, place):
    if place == 0:
        return n[0] - 8.0 * n[1], 16.0 * n[1] - n[0]
    return n[1], -n[1]


def high_parts(p, place):
    if place == 0:
        return 8.0 * p[0] - p[1], 16.0 * p[0] - p[1]
    return -p[0], -p[0]


def halo_share(mid, u, c, g, t_parts, u_parts):
    slope, curve = t_parts
    return STEP_DT * (
        g * curve - c * (u * slope + (HEAT_RATIO - 1.0) * (1.0 + mid) * u_parts[0])
    )


def pack_parts(x):
    nr = x.shape[-1]
    mod4 = lax.broadcasted_iota(jnp.int32, x.shape, 1) % 4
    up1, up2 = pltpu.roll(x, nr - 1, 1), pltpu.roll(x, nr - 2, 1)
    down1, down2 = pltpu.roll(x, 1, 1), pltpu.roll(x, 2, 1)
    above, inner, outer = mod4 >= 2, mod4 == 3, mod4 == 0
    slope = jnp.where(
        above,
        jnp.where(inner, 8.0 * up1, 0.0) - up2,
        down2 - jnp.where(outer, 8.0 * down1, 0.0),
    )
    curve = jnp.where(
        above,
        jnp.where(inner, 16.0 * up1, 0.0) - up2,
        jnp.where(outer, 16.0 * down1, 0.0) - down2,
    )
    return slope, curve


def temperature_kernel(
    vel, temp, base, s_lo, s_hi, a_lo, a_hi, r_left, r_right, cells, r_halo
):
    nt, na, nr = base.shape
    keep, rad, nrad = place()
    join_packs(r_halo, r_left, r_right, keep)
    inv12h, gt, lane = spacings(rad, nrad, nr)
    inv12, g = 1.0 / 12.0, VISCOSITY / 12.0
    turned = cells.reshape(na * nt, nr)
    edge = (lane < 2) | (lane >= nr - 2)
    u_slope, _ = pack_parts(r_halo[1])
    t_slope, t_curve = pack_parts(r_halo[2])
    for t in range(nt):
        even, odd = (nr - 8 * t) % nr, (2 * nr - 8 * t - 4) % nr
        ts = pltpu.roll(t_slope, even, 1) if even else t_slope
        tc = pltpu.roll(t_curve, even, 1) if even else t_curve
        us = pltpu.roll(u_slope, odd, 1) if odd else u_slope
        for j in range(na // 8):
            out = slice(j * 8, j * 8 + 8)
            mid = temp[t, out]
            share = halo_share(mid, vel[2, t, out], inv12, g, (ts[out], tc[out]), (us[out],))
            value = base[t, out] + jnp.where(edge, share, 0.0)
            parts = None
            if t < 2:
                parts = [low_parts((s_lo[f, 0, out], s_lo[f, 1, out]), t) for f in (4, 1)]
            elif t >= nt - 2:
                parts = [
                    high_parts((s_hi[f, 0, out], s_hi[f, 1, out]), nt - 1 - t) for f in (4, 1)
                ]
            if parts is not None:
                value = value + halo_share(mid, vel[0, t, out], inv12h, gt, *parts)
            turned[pl.ds(j * 8 * nt + t, 8, stride=nt), :] = value
    rows, speeds = temp.reshape(nt * na, nr), vel.at[1].reshape(nt * na, nr)
    for a in (0, 1, na - 2, na - 1):
        mid, u = rows[pl.ds(a, nt, stride=na), :], speeds[pl.ds(a, nt, stride=na), :]
        if a < 2:
            parts = [low_parts((a_lo[f, 0], a_lo[f, 1]), a) for f in (4, 2)]
            scale = keep[0]
        else:
            parts = [high_parts((a_hi[f, 0], a_hi[f, 1]), na - 1 - a) for f in (4, 2)]
            scale = keep[1]
        cells[a] = cells[a] + scale * halo_share(mid, u, inv12, g, *parts)


def flow_kernel(
    rho, vel, temp, cells, s_lo, s_hi, a_lo, a_hi, r_left, r_right,
    new_rho, new_vel, new_temp,
    full, flux_t, flux_a, flux_r, press, r_halo,
):
    nt, na, nr = new_rho.shape
    keep, rad, nrad = place()
    for f, ref in enumerate((rho, vel.at[0], vel.at[1], vel.at[2], temp)):
        full[f, 2 : nt + 2, 8 : 8 + na] = ref[...]
    halos = (s_lo, s_hi, a_lo, a_hi, r_left, r_right)
    fill(full, halos, r_halo, keep)

    def products(t, carry):
        mass = 1.0 + full[0, t]
        flux_t[t] = mass * full[1, t]
        press[t] = mass * (1.0 + full[4, t])
        return carry

    lax.fori_loop(0, nt + 4, products, 0)

    def products_in(t, carry):
        mass = 1.0 + full[0, t + 2]
        flux_a[t + 2] = mass * full[2, t + 2]
        flux_r[t] = mass[8 : 8 + na] * full[3, t + 2, 8 : 8 + na]
        return carry

    lax.fori_loop(0, nt, products_in, 0)
    inv12h, gt, lane = spacings(rad, nrad, nr)
    inv12 = 1.0 / 12.0
    turned = cells.reshape(na * nt, nr)

    def step(t, carry):
        even, odd = (nr - 8 * t) % nr, (2 * nr - 8 * t - 4) % nr
        hr, h0, h1, h2, ht = [
            pltpu.roll(r_halo[f // 2], odd if f % 2 else even, 1) for f in range(5)
        ]
        turned_halo = [h0, h1, h2, (1.0 + hr) * h2, (1.0 + hr) * (1.0 + ht)]
        for j in range(na // 8):
            lo, out = 8 + j * 8, slice(j * 8, j * 8 + 8)
            halo = [x[out] for x in turned_halo]
            r0 = full[0, t + 2, lo : lo + 8]
            u = [full[1 + c, t + 2, lo : lo + 8] for c in range(3)]
            w = [u[0] * inv12h, u[1] * inv12, u[2] * inv12]
            scale = 1.0 / (HEAT_RATIO * (1.0 + r0))
            grads = [
                d1(t_shifts(press, t, lo)) * inv12h,
                d1(a_shifts(press, t, lo)) * inv12,
                d1(lane_shifts(press[t + 2, lo : lo + 8], halo[4], lane)) * inv12,
            ]
            for c in range(3):
                ref = full.at[1 + c]
                rate = transport(
                    u[c],
                    t_shifts(ref, t, lo),
                    a_shifts(ref, t, lo),
                    lane_shifts(u[c], halo[c], lane),
                    w,
                    gt,
                )
                new_vel[c, t, out] = u[c] + STEP_DT * (rate - grads[c] * scale)
            loss = (
                d1(t_shifts(flux_t, t, lo)) * inv12h
                + (
                    d1(a_shifts(flux_a, t, lo))
                    + d1(lane_shifts(flux_r[t, out], halo[3], lane))
                )
                * inv12
            )
            new_rho[t, out] = r0 - STEP_DT * loss
            new_temp[t, out] = turned[pl.ds(j * 8 * nt + t, 8, stride=nt), :]
        return carry

    lax.fori_loop(0, nt, step, 0)


def harmonics_kernel(table, spread, out, held, sems):
    sectors, parts, nt, nr = spread.shape
    copies = []
    for p in range(parts):
        x = spread[:, p].reshape(sectors * nt, nr)
        y = jnp.dot(
            table[...], x, precision=lax.Precision.HIGHEST, preferred_element_type=jnp.float32
        )
        held[p] = y.reshape(sectors, HARM // sectors, nr)
        copies.append(pltpu.make_async_copy(held.at[p], out.at[:, p], sems.at[p]))
        copies[p].start()
    for copy in copies:
        copy.wait()


def gather_kernel(parts, out):
    cells, rows, nr = parts.shape
    flat = parts.reshape(cells * rows, nr)
    for k in range(rows):
        out[k] = flat[pl.ds(k, cells, stride=rows), :]


def per_device(table, mass_excess, speed_vector, thermal_excess, energy_release):
    nt, na, nr = mass_excess.shape
    f32 = jnp.float32
    params = pltpu.CompilerParams(vmem_limit_bytes=VMEM_LIMIT)
    sds = jax.ShapeDtypeStruct
    hbm = pl.BlockSpec(memory_space=pltpu.HBM)
    vmem = pl.BlockSpec(memory_space=pltpu.VMEM)
    padded = (nt + 4, na + 16, nr)
    s_lo, s_hi = pl.pallas_call(
        sector_edges_kernel,
        in_specs=[hbm] * 3,
        out_specs=[vmem] * 2,
        out_shape=(sds((5, 2, na, nr), f32), sds((5, 2, na, nr), f32)),
        scratch_shapes=[pltpu.SemaphoreType.DMA((10,))],
        compiler_params=pltpu.CompilerParams(vmem_limit_bytes=54912 * 1024),
        name="sector_edges",
    )(mass_excess, speed_vector, thermal_excess)
    a_lo, a_hi, r_pack = pl.pallas_call(
        tile_edges_kernel,
        in_specs=[vmem] * 4,
        out_specs=[vmem] * 3,
        out_shape=(
            sds((5, 2, nt, nr), f32),
            sds((5, 2, nt, nr), f32),
            sds((PACK_PLANES, na, nr), f32),
        ),
        compiler_params=params,
        name="tile_edges",
    )(s_lo, mass_excess, speed_vector, thermal_excess)

    def ring(axis, up):
        count = lax.axis_size(axis)
        return [(i, (i + (1 if up else -1)) % count) for i in range(count)]

    halos = (
        lax.ppermute(s_hi, "sector", ring("sector", True)),
        lax.ppermute(s_lo, "sector", ring("sector", False)),
        lax.ppermute(a_hi, "ax", ring("ax", True)),
        lax.ppermute(a_lo, "ax", ring("ax", False)),
        lax.ppermute(r_pack, "rad", ring("rad", True)),
        lax.ppermute(r_pack, "rad", ring("rad", False)),
    )
    (base,) = pl.pallas_call(
        inner_kernel,
        in_specs=[vmem] * 3,
        out_specs=[vmem],
        out_shape=(sds((nt, na, nr), f32),),
        scratch_shapes=[pltpu.VMEM((3, *padded), f32)],
        cost_estimate=pl.CostEstimate(
            flops=80 * nt * na * nr, bytes_accessed=24 * nt * na * nr, transcendentals=0
        ),
        compiler_params=params,
        name="inner",
    )(speed_vector, thermal_excess, energy_release)
    (cells,) = pl.pallas_call(
        temperature_kernel,
        in_specs=[vmem] * 9,
        out_specs=[vmem],
        out_shape=(sds((na, nt, nr), f32),),
        scratch_shapes=[pltpu.VMEM((3, na, nr), f32)],
        compiler_params=params,
        name="temperature",
    )(speed_vector, thermal_excess, base, *halos)
    sectors = lax.axis_size("sector")
    rows = HARM // sectors
    share = na // sectors
    spread = lax.all_to_all(
        cells.reshape(sectors, share, nt, nr), "sector", 0, 0, tiled=True
    )
    new_rho, new_vel, new_temp = pl.pallas_call(
        flow_kernel,
        in_specs=[vmem] * 10,
        out_shape=(
            sds((nt, na, nr), f32),
            sds((3, nt, na, nr), f32),
            sds((nt, na, nr), f32),
        ),
        scratch_shapes=[
            pltpu.VMEM((5, *padded), f32),
            pltpu.VMEM(padded, f32),
            pltpu.VMEM(padded, f32),
            pltpu.VMEM((nt, na, nr), f32),
            pltpu.VMEM(padded, f32),
            pltpu.VMEM((3, na, nr), f32),
        ],
        cost_estimate=pl.CostEstimate(
            flops=180 * nt * na * nr, bytes_accessed=44 * nt * na * nr, transcendentals=0
        ),
        compiler_params=params,
        name="flow",
    )(mass_excess, speed_vector, thermal_excess, cells, *halos)
    terms = pl.pallas_call(
        harmonics_kernel,
        in_specs=[vmem] * 2,
        out_specs=hbm,
        out_shape=sds((sectors, share, rows, nr), f32),
        scratch_shapes=[
            pltpu.VMEM((share, sectors, rows, nr), f32),
            pltpu.SemaphoreType.DMA((share,)),
        ],
        compiler_params=params,
        name="harmonics",
    )(table, spread)
    terms = lax.all_to_all(terms, "sector", 0, 0, tiled=True)
    coeffs = pl.pallas_call(
        gather_kernel,
        out_shape=sds((rows, na, nr), f32),
        compiler_params=params,
        name="gather",
    )(terms.reshape(na, rows, nr))
    return (new_rho, new_vel, new_temp, coeffs)


def solution(mesh):
    cell = P("sector", "ax", "rad")
    vector = P(None, "sector", "ax", "rad")

    def run(mass_excess, speed_vector, thermal_excess, energy_release):
        table = jnp.asarray(basis_table(mass_excess.shape[0]))
        return jax.shard_map(
            per_device,
            mesh=mesh,
            in_specs=(P(), cell, vector, cell, cell),
            out_specs=(cell, vector, cell, cell),
            check_vma=False,
        )(table, mass_excess, speed_vector, thermal_excess, energy_release)

    return run
```

```python
import math

import jax
import jax.numpy as jnp
import numpy as np
from jax import lax
from jax.experimental import pallas as pl
from jax.experimental.pallas import tpu as pltpu
from jax.sharding import PartitionSpec as P

HARM = 128
HEAT_RATIO = 1.4
STEP_DT = 0.1
VISCOSITY = 0.1
DIFFUSIVITY = 0.1
VMEM_LIMIT = 16 * 1024 * 1024
PACK_PLANES = 6


def basis_table(ntheta):
    half = HARM // 2
    rows = np.arange(HARM)
    orders = np.where(rows <= half, rows, rows - half)
    phase = orders[:, None] * np.arange(ntheta)[None, :] % ntheta
    angle = phase * (2.0 * math.pi / ntheta)
    values = np.where((rows > half)[:, None], np.sin(angle), np.cos(angle))
    return (values / math.sqrt(ntheta)).astype(np.float32)


def edge_rows(ref, f, first, count, stride):
    lead, rows, lanes = ref.shape[1:]
    return ref.at[f].reshape(lead * rows, lanes).at[pl.ds(first, count, stride=stride), :]


def is_even(axis):
    return lax.axis_index(axis) % 2 == 0


def sector_edges_kernel(rho, vel, temp, far, near, sems):
    nt = rho.shape[0]
    even = is_even("sector")
    near_at, far_at = jnp.where(even, nt - 2, 0), jnp.where(even, 0, nt - 2)
    copies = []
    for f, src in enumerate((rho, vel.at[0], vel.at[1], vel.at[2], temp)):
        for out, at in ((far, far_at), (near, near_at)):
            copies.append(
                pltpu.make_async_copy(src.at[pl.ds(at, 2)], out.at[f], sems.at[len(copies)])
            )
    for copy in copies:
        copy.start()
    for copy in copies:
        copy.wait()


def tile_edges_kernel(after, rho, vel, temp, near, far, r_pack):
    del after
    nt, na, nr = rho.shape
    sources = [rho, vel.at[0], vel.at[1], vel.at[2], temp]
    even = is_even("ax")
    r_pack[3:] = jnp.zeros((r_pack.shape[0] - 3, na, nr), jnp.float32)
    lane = lax.broadcasted_iota(jnp.int32, (na, nr), 1)
    for f, held in enumerate(sources):
        flat = held.reshape(nt * na, nr)
        for side in range(2):
            low = flat[pl.ds(side, nt, stride=na), :]
            high = flat[pl.ds(na - 2 + side, nt, stride=na), :]
            near[f, side] = jnp.where(even, high, low)
            far[f, side] = jnp.where(even, low, high)
        shift = 4 * (f % 2)
        packed = r_pack[f // 2] if f % 2 else jnp.zeros((na, nr), jnp.float32)
        for t in range(nt):
            turn = (8 * t + shift) % nr
            x = held[t]
            turned = pltpu.roll(x, turn, 1) if turn else x
            picked = (lane + 2 - turn) % nr < 4
            packed = jnp.where(picked, turned, packed)
        r_pack[f // 2] = packed


def place():
    ax, rad = lax.axis_index("ax"), lax.axis_index("rad")
    nax, nrad = lax.axis_size("ax"), lax.axis_size("rad")
    keep = [
        jnp.where(c, 1.0, 0.0) for c in (ax > 0, ax < nax - 1, rad > 0, rad < nrad - 1)
    ]
    return keep, rad, nrad


def fill(pad, halos, r_halo, keep):
    s_near, s_far, a_far, a_near, r_left, r_right = halos
    nt, na, nr = pad.shape[1] - 4, pad.shape[2] - 16, pad.shape[3]
    rows = na + 16
    s_even, a_even = is_even("sector"), is_even("ax")
    for f in range(5):
        pad[f, 0:2, 8 : 8 + na] = jnp.where(s_even, s_far[f], s_near[f])
        pad[f, nt + 2 : nt + 4, 8 : 8 + na] = jnp.where(s_even, s_near[f], s_far[f])
        for side in range(2):
            near, far = a_near[f, side], a_far[f, side]
            edge_rows(pad, f, 2 * rows + 6 + side, nt, rows)[...] = (
                jnp.where(a_even, far, near) * keep[0]
            )
            edge_rows(pad, f, 2 * rows + 8 + na + side, nt, rows)[...] = (
                jnp.where(a_even, near, far) * keep[1]
            )
    join_packs(r_halo, r_left, r_right, keep)


def join_packs(r_halo, r_left, r_right, keep):
    mod4 = lax.broadcasted_iota(jnp.int32, r_left.shape[1:], 1) % 4
    for q in range(3):
        r_halo[q] = jnp.where(mod4 < 2, r_right[q] * keep[3], r_left[q] * keep[2])


def spacings(rad, nrad, nr):
    lane = lax.broadcasted_iota(jnp.int32, (8, nr), 1)
    radius = (rad * nr + lane).astype(jnp.float32)
    h = 0.5 + (radius + 0.5) / (nr * nrad)
    return 1.0 / (12.0 * h), VISCOSITY / (12.0 * h * h), lane


def d1(s):
    return 8.0 * (s[2] - s[1]) - (s[3] - s[0])


def lane_shifts(mid, halo, lane):
    nr = mid.shape[-1]
    return [
        pltpu.roll(jnp.where(lane >= nr - 2, halo, mid), 2, 1),
        pltpu.roll(jnp.where(lane == nr - 1, halo, mid), 1, 1),
        pltpu.roll(jnp.where(lane == 0, halo, mid), nr - 1, 1),
        pltpu.roll(jnp.where(lane < 2, halo, mid), nr - 2, 1),
    ]


def t_shifts(ref, t, lo):
    return [ref[t + 2 + d, lo : lo + 8] for d in (-2, -1, 1, 2)]


def a_shifts(ref, t, lo):
    return [ref[t + 2, lo + d : lo + d + 8] for d in (-2, -1, 1, 2)]


def transport(mid, st, sa, sr, w, gt):
    ring1 = (sa[1] + sa[2]) + (sr[1] + sr[2])
    ring2 = (sa[0] + sa[3]) + (sr[0] + sr[3])
    curve_t = 16.0 * (st[1] + st[2]) - 30.0 * mid - (st[0] + st[3])
    curve = 16.0 * ring1 - 60.0 * mid - ring2
    return gt * curve_t + (VISCOSITY / 12.0) * curve - (
        w[0] * d1(st) + w[1] * d1(sa) + w[2] * d1(sr)
    )


def inner_kernel(vel, temp, heat, base, pad):
    nt, na, nr = heat.shape
    rad, nrad = lax.axis_index("rad"), lax.axis_size("rad")
    zeros = jnp.zeros((2, na, nr), jnp.float32)
    for q, ref in enumerate((vel.at[0], vel.at[1], temp)):
        pad[q, 2 : nt + 2, 8 : 8 + na] = ref[...]
        pad[q, 0:2, 8 : 8 + na] = zeros
        pad[q, nt + 2 : nt + 4, 8 : 8 + na] = zeros
        for t in range(nt):
            pad[q, t + 2, 0:8] = zeros[0, 0:8]
            pad[q, t + 2, 8 + na : 16 + na] = zeros[0, 0:8]
    inv12h, gt, lane = spacings(rad, nrad, nr)
    inv12 = 1.0 / 12.0

    def step(t, carry):
        for j in range(na // 8):
            lo, out = 8 + j * 8, slice(j * 8, j * 8 + 8)
            u = [vel[c, t, out] for c in range(3)]
            w = [u[0] * inv12h, u[1] * inv12, u[2] * inv12]
            div = (
                d1(t_shifts(pad.at[0], t, lo)) * inv12h
                + (d1(a_shifts(pad.at[1], t, lo)) + d1(lane_shifts(u[2], 0.0, lane))) * inv12
            )
            mid = temp[t, out]
            rate = transport(
                mid,
                t_shifts(pad.at[2], t, lo),
                a_shifts(pad.at[2], t, lo),
                lane_shifts(mid, 0.0, lane),
                w,
                gt,
            )
            rate = rate - (HEAT_RATIO - 1.0) * (1.0 + mid) * div + heat[t, out]
            base[t, out] = mid + STEP_DT * rate
        return carry

    lax.fori_loop(0, nt, step, 0, unroll=2)


def low_parts(n, place):
    if place == 0:
        return n[0] - 8.0 * n[1], 16.0 * n[1] - n[0]
    return n[1], -n[1]


def high_parts(p, place):
    if place == 0:
        return 8.0 * p[0] - p[1], 16.0 * p[0] - p[1]
    return -p[0], -p[0]


def halo_share(mid, u, c, g, t_parts, u_parts):
    slope, curve = t_parts
    return STEP_DT * (
        g * curve - c * (u * slope + (HEAT_RATIO - 1.0) * (1.0 + mid) * u_parts[0])
    )


def pack_parts(x):
    nr = x.shape[-1]
    mod4 = lax.broadcasted_iota(jnp.int32, x.shape, 1) % 4
    up1, up2 = pltpu.roll(x, nr - 1, 1), pltpu.roll(x, nr - 2, 1)
    down1, down2 = pltpu.roll(x, 1, 1), pltpu.roll(x, 2, 1)
    above, inner, outer = mod4 >= 2, mod4 == 3, mod4 == 0
    slope = jnp.where(
        above,
        jnp.where(inner, 8.0 * up1, 0.0) - up2,
        down2 - jnp.where(outer, 8.0 * down1, 0.0),
    )
    curve = jnp.where(
        above,
        jnp.where(inner, 16.0 * up1, 0.0) - up2,
        jnp.where(outer, 16.0 * down1, 0.0) - down2,
    )
    return slope, curve


def temperature_kernel(
    vel, temp, base, s_near, s_far, a_far, a_near, r_left, r_right, cells, r_halo
):
    nt, na, nr = base.shape
    keep, rad, nrad = place()
    join_packs(r_halo, r_left, r_right, keep)
    inv12h, gt, lane = spacings(rad, nrad, nr)
    inv12, g = 1.0 / 12.0, VISCOSITY / 12.0
    turned = cells.reshape(na * nt, nr)
    s_even, a_even = is_even("sector"), is_even("ax")

    def s_low(f, k, out):
        return jnp.where(s_even, s_far[f, k, out], s_near[f, k, out])

    def s_high(f, k, out):
        return jnp.where(s_even, s_near[f, k, out], s_far[f, k, out])

    def a_low(f, k):
        return jnp.where(a_even, a_far[f, k], a_near[f, k])

    def a_high(f, k):
        return jnp.where(a_even, a_near[f, k], a_far[f, k])

    edge = (lane < 2) | (lane >= nr - 2)
    u_slope, _ = pack_parts(r_halo[1])
    t_slope, t_curve = pack_parts(r_halo[2])
    for t in range(nt):
        even, odd = (nr - 8 * t) % nr, (2 * nr - 8 * t - 4) % nr
        ts = pltpu.roll(t_slope, even, 1) if even else t_slope
        tc = pltpu.roll(t_curve, even, 1) if even else t_curve
        us = pltpu.roll(u_slope, odd, 1) if odd else u_slope
        for j in range(na // 8):
            out = slice(j * 8, j * 8 + 8)
            mid = temp[t, out]
            share = halo_share(mid, vel[2, t, out], inv12, g, (ts[out], tc[out]), (us[out],))
            value = base[t, out] + jnp.where(edge, share, 0.0)
            parts = None
            if t < 2:
                parts = [low_parts([s_low(f, k, out) for k in (0, 1)], t) for f in (4, 1)]
            elif t >= nt - 2:
                parts = [
                    high_parts([s_high(f, k, out) for k in (0, 1)], nt - 1 - t) for f in (4, 1)
                ]
            if parts is not None:
                value = value + halo_share(mid, vel[0, t, out], inv12h, gt, *parts)
            turned[pl.ds(j * 8 * nt + t, 8, stride=nt), :] = value
    rows, speeds = temp.reshape(nt * na, nr), vel.at[1].reshape(nt * na, nr)
    for a in (0, 1, na - 2, na - 1):
        mid, u = rows[pl.ds(a, nt, stride=na), :], speeds[pl.ds(a, nt, stride=na), :]
        if a < 2:
            parts = [low_parts([a_low(f, k) for k in (0, 1)], a) for f in (4, 2)]
            scale = keep[0]
        else:
            parts = [high_parts([a_high(f, k) for k in (0, 1)], na - 1 - a) for f in (4, 2)]
            scale = keep[1]
        cells[a] = cells[a] + scale * halo_share(mid, u, inv12, g, *parts)


def flow_kernel(
    rho, vel, temp, cells, s_near, s_far, a_far, a_near, r_left, r_right,
    new_rho, new_vel, new_temp,
    full, flux_t, flux_a, flux_r, press, r_halo,
):
    nt, na, nr = new_rho.shape
    keep, rad, nrad = place()
    for f, ref in enumerate((rho, vel.at[0], vel.at[1], vel.at[2], temp)):
        full[f, 2 : nt + 2, 8 : 8 + na] = ref[...]
    halos = (s_near, s_far, a_far, a_near, r_left, r_right)
    fill(full, halos, r_halo, keep)

    def products(t, carry):
        mass = 1.0 + full[0, t]
        flux_t[t] = mass * full[1, t]
        press[t] = mass * (1.0 + full[4, t])
        return carry

    lax.fori_loop(0, nt + 4, products, 0)

    def products_in(t, carry):
        mass = 1.0 + full[0, t + 2]
        flux_a[t + 2] = mass * full[2, t + 2]
        flux_r[t] = mass[8 : 8 + na] * full[3, t + 2, 8 : 8 + na]
        return carry

    lax.fori_loop(0, nt, products_in, 0)
    inv12h, gt, lane = spacings(rad, nrad, nr)
    inv12 = 1.0 / 12.0
    turned = cells.reshape(na * nt, nr)

    def step(t, carry):
        even, odd = (nr - 8 * t) % nr, (2 * nr - 8 * t - 4) % nr
        hr, h0, h1, h2, ht = [
            pltpu.roll(r_halo[f // 2], odd if f % 2 else even, 1) for f in range(5)
        ]
        turned_halo = [h0, h1, h2, (1.0 + hr) * h2, (1.0 + hr) * (1.0 + ht)]
        for j in range(na // 8):
            lo, out = 8 + j * 8, slice(j * 8, j * 8 + 8)
            halo = [x[out] for x in turned_halo]
            r0 = full[0, t + 2, lo : lo + 8]
            u = [full[1 + c, t + 2, lo : lo + 8] for c in range(3)]
            w = [u[0] * inv12h, u[1] * inv12, u[2] * inv12]
            scale = 1.0 / (HEAT_RATIO * (1.0 + r0))
            grads = [
                d1(t_shifts(press, t, lo)) * inv12h,
                d1(a_shifts(press, t, lo)) * inv12,
                d1(lane_shifts(press[t + 2, lo : lo + 8], halo[4], lane)) * inv12,
            ]
            for c in range(3):
                ref = full.at[1 + c]
                rate = transport(
                    u[c],
                    t_shifts(ref, t, lo),
                    a_shifts(ref, t, lo),
                    lane_shifts(u[c], halo[c], lane),
                    w,
                    gt,
                )
                new_vel[c, t, out] = u[c] + STEP_DT * (rate - grads[c] * scale)
            loss = (
                d1(t_shifts(flux_t, t, lo)) * inv12h
                + (
                    d1(a_shifts(flux_a, t, lo))
                    + d1(lane_shifts(flux_r[t, out], halo[3], lane))
                )
                * inv12
            )
            new_rho[t, out] = r0 - STEP_DT * loss
            new_temp[t, out] = turned[pl.ds(j * 8 * nt + t, 8, stride=nt), :]
        return carry

    lax.fori_loop(0, nt, step, 0)


def harmonics_kernel(table, spread, out, held, sems):
    sectors, parts, nt, nr = spread.shape
    copies = []
    for p in range(parts):
        x = spread[:, p].reshape(sectors * nt, nr)
        y = jnp.dot(
            table[...], x, precision=lax.Precision.HIGHEST, preferred_element_type=jnp.float32
        )
        held[p] = y.reshape(sectors, HARM // sectors, nr)
        copies.append(pltpu.make_async_copy(held.at[p], out.at[:, p], sems.at[p]))
        copies[p].start()
    for copy in copies:
        copy.wait()


def gather_kernel(parts, out):
    cells, rows, nr = parts.shape
    flat = parts.reshape(cells * rows, nr)
    for k in range(rows):
        out[k] = flat[pl.ds(k, cells, stride=rows), :]


def per_device(table, mass_excess, speed_vector, thermal_excess, energy_release):
    nt, na, nr = mass_excess.shape
    f32 = jnp.float32
    params = pltpu.CompilerParams(vmem_limit_bytes=VMEM_LIMIT)
    sds = jax.ShapeDtypeStruct
    hbm = pl.BlockSpec(memory_space=pltpu.HBM)
    vmem = pl.BlockSpec(memory_space=pltpu.VMEM)
    padded = (nt + 4, na + 16, nr)
    s_far, s_near = pl.pallas_call(
        sector_edges_kernel,
        in_specs=[hbm] * 3,
        out_specs=[vmem] * 2,
        out_shape=(sds((5, 2, na, nr), f32), sds((5, 2, na, nr), f32)),
        scratch_shapes=[pltpu.SemaphoreType.DMA((10,))],
        compiler_params=pltpu.CompilerParams(vmem_limit_bytes=54912 * 1024),
        name="sector_edges",
    )(mass_excess, speed_vector, thermal_excess)
    a_near, a_far, r_pack = pl.pallas_call(
        tile_edges_kernel,
        in_specs=[vmem] * 4,
        out_specs=[vmem] * 3,
        out_shape=(
            sds((5, 2, nt, nr), f32),
            sds((5, 2, nt, nr), f32),
            sds((PACK_PLANES, na, nr), f32),
        ),
        compiler_params=params,
        name="tile_edges",
    )(s_far, mass_excess, speed_vector, thermal_excess)

    def ring(axis, up):
        count = lax.axis_size(axis)
        return [(i, (i + (1 if up else -1)) % count) for i in range(count)]

    def pairs(axis, near):
        count = lax.axis_size(axis)
        return [(i, i ^ 1 if near else (i + (1 if i % 2 else -1)) % count) for i in range(count)]

    s_near = lax.ppermute(s_near, "sector", pairs("sector", True))
    s_far = lax.ppermute(s_far, "sector", pairs("sector", False))
    a_far = lax.ppermute(a_far, "ax", pairs("ax", False))
    a_near = lax.ppermute(a_near, "ax", pairs("ax", True))
    r_left = lax.ppermute(r_pack, "rad", ring("rad", True))
    r_right = lax.ppermute(r_pack, "rad", ring("rad", False))
    halos = (s_near, s_far, a_far, a_near, r_left, r_right)
    (base,) = pl.pallas_call(
        inner_kernel,
        in_specs=[vmem] * 3,
        out_specs=[vmem],
        out_shape=(sds((nt, na, nr), f32),),
        scratch_shapes=[pltpu.VMEM((3, *padded), f32)],
        cost_estimate=pl.CostEstimate(
            flops=80 * nt * na * nr, bytes_accessed=24 * nt * na * nr, transcendentals=0
        ),
        compiler_params=params,
        name="inner",
    )(speed_vector, thermal_excess, energy_release)
    (cells,) = pl.pallas_call(
        temperature_kernel,
        in_specs=[vmem] * 9,
        out_specs=[vmem],
        out_shape=(sds((na, nt, nr), f32),),
        scratch_shapes=[pltpu.VMEM((3, na, nr), f32)],
        compiler_params=params,
        name="temperature",
    )(speed_vector, thermal_excess, base, *halos)
    sectors = lax.axis_size("sector")
    rows = HARM // sectors
    share = na // sectors
    spread = lax.all_to_all(
        cells.reshape(sectors, share, nt, nr), "sector", 0, 0, tiled=True
    )
    new_rho, new_vel, new_temp = pl.pallas_call(
        flow_kernel,
        in_specs=[vmem] * 10,
        out_shape=(
            sds((nt, na, nr), f32),
            sds((3, nt, na, nr), f32),
            sds((nt, na, nr), f32),
        ),
        scratch_shapes=[
            pltpu.VMEM((5, *padded), f32),
            pltpu.VMEM(padded, f32),
            pltpu.VMEM(padded, f32),
            pltpu.VMEM((nt, na, nr), f32),
            pltpu.VMEM(padded, f32),
            pltpu.VMEM((3, na, nr), f32),
        ],
        cost_estimate=pl.CostEstimate(
            flops=180 * nt * na * nr, bytes_accessed=44 * nt * na * nr, transcendentals=0
        ),
        compiler_params=params,
        name="flow",
    )(mass_excess, speed_vector, thermal_excess, cells, *halos)
    terms = pl.pallas_call(
        harmonics_kernel,
        in_specs=[vmem] * 2,
        out_specs=hbm,
        out_shape=sds((sectors, share, rows, nr), f32),
        scratch_shapes=[
            pltpu.VMEM((share, sectors, rows, nr), f32),
            pltpu.SemaphoreType.DMA((share,)),
        ],
        compiler_params=params,
        name="harmonics",
    )(table, spread)
    terms = lax.all_to_all(terms, "sector", 0, 0, tiled=True)
    coeffs = pl.pallas_call(
        gather_kernel,
        out_shape=sds((rows, na, nr), f32),
        compiler_params=params,
        name="gather",
    )(terms.reshape(na, rows, nr))
    return (new_rho, new_vel, new_temp, coeffs)


def solution(mesh):
    cell = P("sector", "ax", "rad")
    vector = P(None, "sector", "ax", "rad")

    def run(mass_excess, speed_vector, thermal_excess, energy_release):
        table = jnp.asarray(basis_table(mass_excess.shape[0]))
        return jax.shard_map(
            per_device,
            mesh=mesh,
            in_specs=(P(), cell, vector, cell, cell),
            out_specs=(cell, vector, cell, cell),
            check_vma=False,
        )(table, mass_excess, speed_vector, thermal_excess, energy_release)

    return run
```

```python
import math

import jax
import jax.numpy as jnp
import numpy as np
from jax import lax
from jax.experimental import pallas as pl
from jax.experimental.pallas import tpu as pltpu
from jax.sharding import PartitionSpec as P

HARM = 128
HEAT_RATIO = 1.4
STEP_DT = 0.1
VISCOSITY = 0.1
DIFFUSIVITY = 0.1
VMEM_LIMIT = 16 * 1024 * 1024
PACK_PLANES = 6


def basis_table(ntheta):
    half = HARM // 2
    rows = np.arange(HARM)
    orders = np.where(rows <= half, rows, rows - half)
    phase = orders[:, None] * np.arange(ntheta)[None, :] % ntheta
    angle = phase * (2.0 * math.pi / ntheta)
    values = np.where((rows > half)[:, None], np.sin(angle), np.cos(angle))
    return (values / math.sqrt(ntheta)).astype(np.float32)


def edge_rows(ref, f, first, count, stride):
    lead, rows, lanes = ref.shape[1:]
    return ref.at[f].reshape(lead * rows, lanes).at[pl.ds(first, count, stride=stride), :]


def is_even(axis):
    return lax.axis_index(axis) % 2 == 0


def sector_edges_kernel(rho, vel, temp, far, near, sems):
    nt = rho.shape[0]
    even = is_even("sector")
    near_at, far_at = jnp.where(even, nt - 2, 0), jnp.where(even, 0, nt - 2)
    copies = []
    for f, src in enumerate((rho, vel.at[0], vel.at[1], vel.at[2], temp)):
        for out, at in ((far, far_at), (near, near_at)):
            copies.append(
                pltpu.make_async_copy(src.at[pl.ds(at, 2)], out.at[f], sems.at[len(copies)])
            )
    for copy in copies:
        copy.start()
    for copy in copies:
        copy.wait()


def tile_edges_kernel(after, rho, vel, temp, near, far, r_pack, r_copy):
    del after
    nt, na, nr = rho.shape
    sources = [rho, vel.at[0], vel.at[1], vel.at[2], temp]
    even = is_even("ax")
    for ref in (r_pack, r_copy):
        if ref.shape[0] > 3:
            ref[3:] = jnp.zeros((ref.shape[0] - 3, na, nr), jnp.float32)
    lane = lax.broadcasted_iota(jnp.int32, (na, nr), 1)
    for f, held in enumerate(sources):
        flat = held.reshape(nt * na, nr)
        for side in range(2):
            low = flat[pl.ds(side, nt, stride=na), :]
            high = flat[pl.ds(na - 2 + side, nt, stride=na), :]
            near[f, side] = jnp.where(even, high, low)
            far[f, side] = jnp.where(even, low, high)
        shift = 4 * (f % 2)
        packed = r_pack[f // 2] if f % 2 else jnp.zeros((na, nr), jnp.float32)
        for t in range(nt):
            turn = (8 * t + shift) % nr
            x = held[t]
            turned = pltpu.roll(x, turn, 1) if turn else x
            picked = (lane + 2 - turn) % nr < 4
            packed = jnp.where(picked, turned, packed)
        r_pack[f // 2] = packed
        r_copy[f // 2] = packed


def place():
    ax, rad = lax.axis_index("ax"), lax.axis_index("rad")
    nax, nrad = lax.axis_size("ax"), lax.axis_size("rad")
    keep = [
        jnp.where(c, 1.0, 0.0) for c in (ax > 0, ax < nax - 1, rad > 0, rad < nrad - 1)
    ]
    return keep, rad, nrad


def fill(pad, halos, r_halo, keep):
    s_near, s_far, a_far, a_near, r_right, r_left = halos
    nt, na, nr = pad.shape[1] - 4, pad.shape[2] - 16, pad.shape[3]
    rows = na + 16
    s_even, a_even = is_even("sector"), is_even("ax")
    for f in range(5):
        pad[f, 0:2, 8 : 8 + na] = jnp.where(s_even, s_far[f], s_near[f])
        pad[f, nt + 2 : nt + 4, 8 : 8 + na] = jnp.where(s_even, s_near[f], s_far[f])
        for side in range(2):
            near, far = a_near[f, side], a_far[f, side]
            edge_rows(pad, f, 2 * rows + 6 + side, nt, rows)[...] = (
                jnp.where(a_even, far, near) * keep[0]
            )
            edge_rows(pad, f, 2 * rows + 8 + na + side, nt, rows)[...] = (
                jnp.where(a_even, near, far) * keep[1]
            )
    join_packs(r_halo, r_left, r_right, keep)


def join_packs(r_halo, r_left, r_right, keep):
    mod4 = lax.broadcasted_iota(jnp.int32, r_left.shape[1:], 1) % 4
    for q in range(3):
        r_halo[q] = jnp.where(mod4 < 2, r_right[q] * keep[3], r_left[q] * keep[2])


def spacings(rad, nrad, nr):
    lane = lax.broadcasted_iota(jnp.int32, (8, nr), 1)
    radius = (rad * nr + lane).astype(jnp.float32)
    h = 0.5 + (radius + 0.5) / (nr * nrad)
    return 1.0 / (12.0 * h), VISCOSITY / (12.0 * h * h), lane


def d1(s):
    return 8.0 * (s[2] - s[1]) - (s[3] - s[0])


def lane_shifts(mid, halo, lane):
    nr = mid.shape[-1]
    return [
        pltpu.roll(jnp.where(lane >= nr - 2, halo, mid), 2, 1),
        pltpu.roll(jnp.where(lane == nr - 1, halo, mid), 1, 1),
        pltpu.roll(jnp.where(lane == 0, halo, mid), nr - 1, 1),
        pltpu.roll(jnp.where(lane < 2, halo, mid), nr - 2, 1),
    ]


def t_shifts(ref, t, lo):
    return [ref[t + 2 + d, lo : lo + 8] for d in (-2, -1, 1, 2)]


def a_shifts(ref, t, lo):
    return [ref[t + 2, lo + d : lo + d + 8] for d in (-2, -1, 1, 2)]


def transport(mid, st, sa, sr, w, gt):
    ring1 = (sa[1] + sa[2]) + (sr[1] + sr[2])
    ring2 = (sa[0] + sa[3]) + (sr[0] + sr[3])
    curve_t = 16.0 * (st[1] + st[2]) - 30.0 * mid - (st[0] + st[3])
    curve = 16.0 * ring1 - 60.0 * mid - ring2
    return gt * curve_t + (VISCOSITY / 12.0) * curve - (
        w[0] * d1(st) + w[1] * d1(sa) + w[2] * d1(sr)
    )


def inner_kernel(vel, temp, heat, base, pad):
    nt, na, nr = heat.shape
    rad, nrad = lax.axis_index("rad"), lax.axis_size("rad")
    zeros = jnp.zeros((2, na, nr), jnp.float32)
    for q, ref in enumerate((vel.at[0], vel.at[1], temp)):
        pad[q, 2 : nt + 2, 8 : 8 + na] = ref[...]
        pad[q, 0:2, 8 : 8 + na] = zeros
        pad[q, nt + 2 : nt + 4, 8 : 8 + na] = zeros
        for t in range(nt):
            pad[q, t + 2, 0:8] = zeros[0, 0:8]
            pad[q, t + 2, 8 + na : 16 + na] = zeros[0, 0:8]
    inv12h, gt, lane = spacings(rad, nrad, nr)
    inv12 = 1.0 / 12.0

    def step(t, carry):
        for j in range(na // 8):
            lo, out = 8 + j * 8, slice(j * 8, j * 8 + 8)
            u = [vel[c, t, out] for c in range(3)]
            w = [u[0] * inv12h, u[1] * inv12, u[2] * inv12]
            div = (
                d1(t_shifts(pad.at[0], t, lo)) * inv12h
                + (d1(a_shifts(pad.at[1], t, lo)) + d1(lane_shifts(u[2], 0.0, lane))) * inv12
            )
            mid = temp[t, out]
            rate = transport(
                mid,
                t_shifts(pad.at[2], t, lo),
                a_shifts(pad.at[2], t, lo),
                lane_shifts(mid, 0.0, lane),
                w,
                gt,
            )
            rate = rate - (HEAT_RATIO - 1.0) * (1.0 + mid) * div + heat[t, out]
            base[t, out] = mid + STEP_DT * rate
        return carry

    lax.fori_loop(0, nt, step, 0, unroll=2)


def low_parts(n, place):
    if place == 0:
        return n[0] - 8.0 * n[1], 16.0 * n[1] - n[0]
    return n[1], -n[1]


def high_parts(p, place):
    if place == 0:
        return 8.0 * p[0] - p[1], 16.0 * p[0] - p[1]
    return -p[0], -p[0]


def halo_share(mid, u, c, g, t_parts, u_parts):
    slope, curve = t_parts
    return STEP_DT * (
        g * curve - c * (u * slope + (HEAT_RATIO - 1.0) * (1.0 + mid) * u_parts[0])
    )


def pack_parts(x):
    nr = x.shape[-1]
    mod4 = lax.broadcasted_iota(jnp.int32, x.shape, 1) % 4
    up1, up2 = pltpu.roll(x, nr - 1, 1), pltpu.roll(x, nr - 2, 1)
    down1, down2 = pltpu.roll(x, 1, 1), pltpu.roll(x, 2, 1)
    above, inner, outer = mod4 >= 2, mod4 == 3, mod4 == 0
    slope = jnp.where(
        above,
        jnp.where(inner, 8.0 * up1, 0.0) - up2,
        down2 - jnp.where(outer, 8.0 * down1, 0.0),
    )
    curve = jnp.where(
        above,
        jnp.where(inner, 16.0 * up1, 0.0) - up2,
        jnp.where(outer, 16.0 * down1, 0.0) - down2,
    )
    return slope, curve


def temperature_kernel(
    vel, temp, base, s_near, s_far, a_far, a_near, r_right, r_left, cells, r_halo
):
    nt, na, nr = base.shape
    keep, rad, nrad = place()
    join_packs(r_halo, r_left, r_right, keep)
    inv12h, gt, lane = spacings(rad, nrad, nr)
    inv12, g = 1.0 / 12.0, VISCOSITY / 12.0
    turned = cells.reshape(na * nt, nr)
    s_even, a_even = is_even("sector"), is_even("ax")

    def s_low(f, k, out):
        return jnp.where(s_even, s_far[f, k, out], s_near[f, k, out])

    def s_high(f, k, out):
        return jnp.where(s_even, s_near[f, k, out], s_far[f, k, out])

    def a_low(f, k):
        return jnp.where(a_even, a_far[f, k], a_near[f, k])

    def a_high(f, k):
        return jnp.where(a_even, a_near[f, k], a_far[f, k])

    edge = (lane < 2) | (lane >= nr - 2)
    u_slope, _ = pack_parts(r_halo[1])
    t_slope, t_curve = pack_parts(r_halo[2])
    for t in range(nt):
        even, odd = (nr - 8 * t) % nr, (2 * nr - 8 * t - 4) % nr
        ts = pltpu.roll(t_slope, even, 1) if even else t_slope
        tc = pltpu.roll(t_curve, even, 1) if even else t_curve
        us = pltpu.roll(u_slope, odd, 1) if odd else u_slope
        for j in range(na // 8):
            out = slice(j * 8, j * 8 + 8)
            mid = temp[t, out]
            share = halo_share(mid, vel[2, t, out], inv12, g, (ts[out], tc[out]), (us[out],))
            value = base[t, out] + jnp.where(edge, share, 0.0)
            parts = None
            if t < 2:
                parts = [low_parts([s_low(f, k, out) for k in (0, 1)], t) for f in (4, 1)]
            elif t >= nt - 2:
                parts = [
                    high_parts([s_high(f, k, out) for k in (0, 1)], nt - 1 - t) for f in (4, 1)
                ]
            if parts is not None:
                value = value + halo_share(mid, vel[0, t, out], inv12h, gt, *parts)
            turned[pl.ds(j * 8 * nt + t, 8, stride=nt), :] = value
    rows, speeds = temp.reshape(nt * na, nr), vel.at[1].reshape(nt * na, nr)
    for a in (0, 1, na - 2, na - 1):
        mid, u = rows[pl.ds(a, nt, stride=na), :], speeds[pl.ds(a, nt, stride=na), :]
        if a < 2:
            parts = [low_parts([a_low(f, k) for k in (0, 1)], a) for f in (4, 2)]
            scale = keep[0]
        else:
            parts = [high_parts([a_high(f, k) for k in (0, 1)], na - 1 - a) for f in (4, 2)]
            scale = keep[1]
        cells[a] = cells[a] + scale * halo_share(mid, u, inv12, g, *parts)


def flow_kernel(
    rho, vel, temp, cells, s_near, s_far, a_far, a_near, r_right, r_left,
    new_rho, new_vel, new_temp,
    full, flux_t, flux_a, flux_r, press, r_halo,
):
    nt, na, nr = new_rho.shape
    keep, rad, nrad = place()
    for f, ref in enumerate((rho, vel.at[0], vel.at[1], vel.at[2], temp)):
        full[f, 2 : nt + 2, 8 : 8 + na] = ref[...]
    halos = (s_near, s_far, a_far, a_near, r_right, r_left)
    fill(full, halos, r_halo, keep)

    def products(t, carry):
        mass = 1.0 + full[0, t]
        flux_t[t] = mass * full[1, t]
        press[t] = mass * (1.0 + full[4, t])
        return carry

    lax.fori_loop(0, nt + 4, products, 0)

    def products_in(t, carry):
        mass = 1.0 + full[0, t + 2]
        flux_a[t + 2] = mass * full[2, t + 2]
        flux_r[t] = mass[8 : 8 + na] * full[3, t + 2, 8 : 8 + na]
        return carry

    lax.fori_loop(0, nt, products_in, 0)
    inv12h, gt, lane = spacings(rad, nrad, nr)
    inv12 = 1.0 / 12.0
    turned = cells.reshape(na * nt, nr)

    def step(t, carry):
        even, odd = (nr - 8 * t) % nr, (2 * nr - 8 * t - 4) % nr
        hr, h0, h1, h2, ht = [
            pltpu.roll(r_halo[f // 2], odd if f % 2 else even, 1) for f in range(5)
        ]
        turned_halo = [h0, h1, h2, (1.0 + hr) * h2, (1.0 + hr) * (1.0 + ht)]
        for j in range(na // 8):
            lo, out = 8 + j * 8, slice(j * 8, j * 8 + 8)
            halo = [x[out] for x in turned_halo]
            r0 = full[0, t + 2, lo : lo + 8]
            u = [full[1 + c, t + 2, lo : lo + 8] for c in range(3)]
            w = [u[0] * inv12h, u[1] * inv12, u[2] * inv12]
            scale = 1.0 / (HEAT_RATIO * (1.0 + r0))
            grads = [
                d1(t_shifts(press, t, lo)) * inv12h,
                d1(a_shifts(press, t, lo)) * inv12,
                d1(lane_shifts(press[t + 2, lo : lo + 8], halo[4], lane)) * inv12,
            ]
            for c in range(3):
                ref = full.at[1 + c]
                rate = transport(
                    u[c],
                    t_shifts(ref, t, lo),
                    a_shifts(ref, t, lo),
                    lane_shifts(u[c], halo[c], lane),
                    w,
                    gt,
                )
                new_vel[c, t, out] = u[c] + STEP_DT * (rate - grads[c] * scale)
            loss = (
                d1(t_shifts(flux_t, t, lo)) * inv12h
                + (
                    d1(a_shifts(flux_a, t, lo))
                    + d1(lane_shifts(flux_r[t, out], halo[3], lane))
                )
                * inv12
            )
            new_rho[t, out] = r0 - STEP_DT * loss
            new_temp[t, out] = turned[pl.ds(j * 8 * nt + t, 8, stride=nt), :]
        return carry

    lax.fori_loop(0, nt, step, 0)


def harmonics_kernel(table, spread, out, held, sems):
    sectors, parts, nt, nr = spread.shape
    copies = []
    for p in range(parts):
        x = spread[:, p].reshape(sectors * nt, nr)
        y = jnp.dot(
            table[...], x, precision=lax.Precision.HIGHEST, preferred_element_type=jnp.float32
        )
        held[p] = y.reshape(sectors, HARM // sectors, nr)
        copies.append(pltpu.make_async_copy(held.at[p], out.at[:, p], sems.at[p]))
        copies[p].start()
    for copy in copies:
        copy.wait()


def gather_kernel(parts, out):
    cells, rows, nr = parts.shape
    flat = parts.reshape(cells * rows, nr)
    for k in range(rows):
        out[k] = flat[pl.ds(k, cells, stride=rows), :]


def per_device(table, mass_excess, speed_vector, thermal_excess, energy_release):
    nt, na, nr = mass_excess.shape
    f32 = jnp.float32
    params = pltpu.CompilerParams(vmem_limit_bytes=VMEM_LIMIT)
    sds = jax.ShapeDtypeStruct
    hbm = pl.BlockSpec(memory_space=pltpu.HBM)
    vmem = pl.BlockSpec(memory_space=pltpu.VMEM)
    padded = (nt + 4, na + 16, nr)
    s_far, s_near = pl.pallas_call(
        sector_edges_kernel,
        in_specs=[hbm] * 3,
        out_specs=[vmem] * 2,
        out_shape=(sds((5, 2, na, nr), f32), sds((5, 2, na, nr), f32)),
        scratch_shapes=[pltpu.SemaphoreType.DMA((10,))],
        compiler_params=pltpu.CompilerParams(vmem_limit_bytes=54912 * 1024),
        name="sector_edges",
    )(mass_excess, speed_vector, thermal_excess)
    a_near, a_far, r_pack, r_copy = pl.pallas_call(
        tile_edges_kernel,
        in_specs=[vmem] * 4,
        out_specs=[vmem] * 4,
        out_shape=(
            sds((5, 2, nt, nr), f32),
            sds((5, 2, nt, nr), f32),
            sds((3, na, nr), f32),
            sds((PACK_PLANES, na, nr), f32),
        ),
        compiler_params=params,
        name="tile_edges",
    )(s_far, mass_excess, speed_vector, thermal_excess)

    def ring(axis, up):
        count = lax.axis_size(axis)
        return [(i, (i + (1 if up else -1)) % count) for i in range(count)]

    def pairs(axis, near):
        count = lax.axis_size(axis)
        return [(i, i ^ 1 if near else (i + (1 if i % 2 else -1)) % count) for i in range(count)]

    s_near = lax.ppermute(s_near, "sector", pairs("sector", True))
    s_far = lax.ppermute(s_far, "sector", pairs("sector", False))
    a_far = lax.ppermute(a_far, "ax", pairs("ax", False))
    a_near = lax.ppermute(a_near, "ax", pairs("ax", True))
    r_left = lax.ppermute(r_pack, "rad", ring("rad", True))
    r_right = lax.ppermute(r_copy, "rad", ring("rad", False))
    halos = (s_near, s_far, a_far, a_near, r_right, r_left)
    (base,) = pl.pallas_call(
        inner_kernel,
        in_specs=[vmem] * 3,
        out_specs=[vmem],
        out_shape=(sds((nt, na, nr), f32),),
        scratch_shapes=[pltpu.VMEM((3, *padded), f32)],
        cost_estimate=pl.CostEstimate(
            flops=80 * nt * na * nr, bytes_accessed=24 * nt * na * nr, transcendentals=0
        ),
        compiler_params=params,
        name="inner",
    )(speed_vector, thermal_excess, energy_release)
    (cells,) = pl.pallas_call(
        temperature_kernel,
        in_specs=[vmem] * 9,
        out_specs=[vmem],
        out_shape=(sds((na, nt, nr), f32),),
        scratch_shapes=[pltpu.VMEM((3, na, nr), f32)],
        compiler_params=params,
        name="temperature",
    )(speed_vector, thermal_excess, base, *halos)
    sectors = lax.axis_size("sector")
    rows = HARM // sectors
    share = na // sectors
    spread = lax.all_to_all(
        cells.reshape(sectors, share, nt, nr), "sector", 0, 0, tiled=True
    )
    new_rho, new_vel, new_temp = pl.pallas_call(
        flow_kernel,
        in_specs=[vmem] * 10,
        out_shape=(
            sds((nt, na, nr), f32),
            sds((3, nt, na, nr), f32),
            sds((nt, na, nr), f32),
        ),
        scratch_shapes=[
            pltpu.VMEM((5, *padded), f32),
            pltpu.VMEM(padded, f32),
            pltpu.VMEM(padded, f32),
            pltpu.VMEM((nt, na, nr), f32),
            pltpu.VMEM(padded, f32),
            pltpu.VMEM((3, na, nr), f32),
        ],
        cost_estimate=pl.CostEstimate(
            flops=180 * nt * na * nr, bytes_accessed=44 * nt * na * nr, transcendentals=0
        ),
        compiler_params=params,
        name="flow",
    )(mass_excess, speed_vector, thermal_excess, cells, *halos)
    terms = pl.pallas_call(
        harmonics_kernel,
        in_specs=[vmem] * 2,
        out_specs=hbm,
        out_shape=sds((sectors, share, rows, nr), f32),
        scratch_shapes=[
            pltpu.VMEM((share, sectors, rows, nr), f32),
            pltpu.SemaphoreType.DMA((share,)),
        ],
        compiler_params=params,
        name="harmonics",
    )(table, spread)
    terms = lax.all_to_all(terms, "sector", 0, 0, tiled=True)
    coeffs = pl.pallas_call(
        gather_kernel,
        out_shape=sds((rows, na, nr), f32),
        compiler_params=params,
        name="gather",
    )(terms.reshape(na, rows, nr))
    return (new_rho, new_vel, new_temp, coeffs)


def solution(mesh):
    cell = P("sector", "ax", "rad")
    vector = P(None, "sector", "ax", "rad")

    def run(mass_excess, speed_vector, thermal_excess, energy_release):
        table = jnp.asarray(basis_table(mass_excess.shape[0]))
        return jax.shard_map(
            per_device,
            mesh=mesh,
            in_specs=(P(), cell, vector, cell, cell),
            out_specs=(cell, vector, cell, cell),
            check_vma=False,
        )(table, mass_excess, speed_vector, thermal_excess, energy_release)

    return run
```

```python
import math

import jax
import jax.numpy as jnp
import numpy as np
from jax import lax
from jax.experimental import pallas as pl
from jax.experimental.pallas import tpu as pltpu
from jax.sharding import PartitionSpec as P

HARM = 128
HEAT_RATIO = 1.4
STEP_DT = 0.1
VISCOSITY = 0.1
DIFFUSIVITY = 0.1
VMEM_LIMIT = 16 * 1024 * 1024
PACK_PLANES = 6


def basis_table(ntheta):
    half = HARM // 2
    rows = np.arange(HARM)
    orders = np.where(rows <= half, rows, rows - half)
    phase = orders[:, None] * np.arange(ntheta)[None, :] % ntheta
    angle = phase * (2.0 * math.pi / ntheta)
    values = np.where((rows > half)[:, None], np.sin(angle), np.cos(angle))
    return (values / math.sqrt(ntheta)).astype(np.float32)


def edge_rows(ref, f, first, count, stride):
    lead, rows, lanes = ref.shape[1:]
    return ref.at[f].reshape(lead * rows, lanes).at[pl.ds(first, count, stride=stride), :]


def is_even(axis):
    return lax.axis_index(axis) % 2 == 0


def sector_edges_kernel(rho, vel, temp, far, near, sems):
    nt = rho.shape[0]
    even = is_even("sector")
    near_at, far_at = jnp.where(even, nt - 2, 0), jnp.where(even, 0, nt - 2)
    copies = []
    for f, src in enumerate((rho, vel.at[0], vel.at[1], vel.at[2], temp)):
        for out, at in ((far, far_at), (near, near_at)):
            copies.append(
                pltpu.make_async_copy(src.at[pl.ds(at, 2)], out.at[f], sems.at[len(copies)])
            )
    for copy in copies:
        copy.start()
    for copy in copies:
        copy.wait()


def tile_edges_kernel(after, rho, vel, temp, near, far, r_pack):
    del after
    nt, na, nr = rho.shape
    sources = [rho, vel.at[0], vel.at[1], vel.at[2], temp]
    even = is_even("ax")
    r_pack[3:] = jnp.zeros((r_pack.shape[0] - 3, na, nr), jnp.float32)
    lane = lax.broadcasted_iota(jnp.int32, (na, nr), 1)
    for f, held in enumerate(sources):
        flat = held.reshape(nt * na, nr)
        for side in range(2):
            low = flat[pl.ds(side, nt, stride=na), :]
            high = flat[pl.ds(na - 2 + side, nt, stride=na), :]
            near[f, side] = jnp.where(even, high, low)
            far[f, side] = jnp.where(even, low, high)
        shift = 4 * (f % 2)
        packed = r_pack[f // 2] if f % 2 else jnp.zeros((na, nr), jnp.float32)
        for t in range(nt):
            turn = (8 * t + shift) % nr
            x = held[t]
            turned = pltpu.roll(x, turn, 1) if turn else x
            picked = (lane + 2 - turn) % nr < 4
            packed = jnp.where(picked, turned, packed)
        r_pack[f // 2] = packed


def place():
    ax, rad = lax.axis_index("ax"), lax.axis_index("rad")
    nax, nrad = lax.axis_size("ax"), lax.axis_size("rad")
    keep = [
        jnp.where(c, 1.0, 0.0) for c in (ax > 0, ax < nax - 1, rad > 0, rad < nrad - 1)
    ]
    return keep, rad, nrad


def fill(pad, halos, r_halo, keep):
    s_near, s_far, a_far, a_near, r_left, r_right = halos
    nt, na, nr = pad.shape[1] - 4, pad.shape[2] - 16, pad.shape[3]
    rows = na + 16
    s_even, a_even = is_even("sector"), is_even("ax")
    for f in range(5):
        pad[f, 0:2, 8 : 8 + na] = jnp.where(s_even, s_far[f], s_near[f])
        pad[f, nt + 2 : nt + 4, 8 : 8 + na] = jnp.where(s_even, s_near[f], s_far[f])
        for side in range(2):
            near, far = a_near[f, side], a_far[f, side]
            edge_rows(pad, f, 2 * rows + 6 + side, nt, rows)[...] = (
                jnp.where(a_even, far, near) * keep[0]
            )
            edge_rows(pad, f, 2 * rows + 8 + na + side, nt, rows)[...] = (
                jnp.where(a_even, near, far) * keep[1]
            )
    join_packs(r_halo, r_left, r_right, keep)


def join_packs(r_halo, r_left, r_right, keep):
    mod4 = lax.broadcasted_iota(jnp.int32, r_left.shape[1:], 1) % 4
    for q in range(3):
        r_halo[q] = jnp.where(mod4 < 2, r_right[q] * keep[3], r_left[q] * keep[2])


def spacings(rad, nrad, nr):
    lane = lax.broadcasted_iota(jnp.int32, (8, nr), 1)
    radius = (rad * nr + lane).astype(jnp.float32)
    h = 0.5 + (radius + 0.5) / (nr * nrad)
    return 1.0 / (12.0 * h), VISCOSITY / (12.0 * h * h), lane


def d1(s):
    return 8.0 * (s[2] - s[1]) - (s[3] - s[0])


def lane_shifts(mid, halo, lane):
    nr = mid.shape[-1]
    return [
        pltpu.roll(jnp.where(lane >= nr - 2, halo, mid), 2, 1),
        pltpu.roll(jnp.where(lane == nr - 1, halo, mid), 1, 1),
        pltpu.roll(jnp.where(lane == 0, halo, mid), nr - 1, 1),
        pltpu.roll(jnp.where(lane < 2, halo, mid), nr - 2, 1),
    ]


def t_shifts(ref, t, lo):
    return [ref[t + 2 + d, lo : lo + 8] for d in (-2, -1, 1, 2)]


def a_shifts(ref, t, lo):
    return [ref[t + 2, lo + d : lo + d + 8] for d in (-2, -1, 1, 2)]


def transport(mid, st, sa, sr, w, gt):
    ring1 = (sa[1] + sa[2]) + (sr[1] + sr[2])
    ring2 = (sa[0] + sa[3]) + (sr[0] + sr[3])
    curve_t = 16.0 * (st[1] + st[2]) - 30.0 * mid - (st[0] + st[3])
    curve = 16.0 * ring1 - 60.0 * mid - ring2
    return gt * curve_t + (VISCOSITY / 12.0) * curve - (
        w[0] * d1(st) + w[1] * d1(sa) + w[2] * d1(sr)
    )


def inner_kernel(vel, temp, heat, base, pad):
    nt, na, nr = heat.shape
    rad, nrad = lax.axis_index("rad"), lax.axis_size("rad")
    zeros = jnp.zeros((2, na, nr), jnp.float32)
    for q, ref in enumerate((vel.at[0], vel.at[1], temp)):
        pad[q, 2 : nt + 2, 8 : 8 + na] = ref[...]
        pad[q, 0:2, 8 : 8 + na] = zeros
        pad[q, nt + 2 : nt + 4, 8 : 8 + na] = zeros
        for t in range(nt):
            pad[q, t + 2, 0:8] = zeros[0, 0:8]
            pad[q, t + 2, 8 + na : 16 + na] = zeros[0, 0:8]
    inv12h, gt, lane = spacings(rad, nrad, nr)
    inv12 = 1.0 / 12.0

    def step(t, carry):
        for j in range(na // 8):
            lo, out = 8 + j * 8, slice(j * 8, j * 8 + 8)
            u = [vel[c, t, out] for c in range(3)]
            w = [u[0] * inv12h, u[1] * inv12, u[2] * inv12]
            div = (
                d1(t_shifts(pad.at[0], t, lo)) * inv12h
                + (d1(a_shifts(pad.at[1], t, lo)) + d1(lane_shifts(u[2], 0.0, lane))) * inv12
            )
            mid = temp[t, out]
            rate = transport(
                mid,
                t_shifts(pad.at[2], t, lo),
                a_shifts(pad.at[2], t, lo),
                lane_shifts(mid, 0.0, lane),
                w,
                gt,
            )
            rate = rate - (HEAT_RATIO - 1.0) * (1.0 + mid) * div + heat[t, out]
            base[t, out] = mid + STEP_DT * rate
        return carry

    lax.fori_loop(0, nt, step, 0, unroll=2)


def low_parts(n, place):
    if place == 0:
        return n[0] - 8.0 * n[1], 16.0 * n[1] - n[0]
    return n[1], -n[1]


def high_parts(p, place):
    if place == 0:
        return 8.0 * p[0] - p[1], 16.0 * p[0] - p[1]
    return -p[0], -p[0]


def halo_share(mid, u, c, g, t_parts, u_parts):
    slope, curve = t_parts
    return STEP_DT * (
        g * curve - c * (u * slope + (HEAT_RATIO - 1.0) * (1.0 + mid) * u_parts[0])
    )


def pack_parts(x):
    nr = x.shape[-1]
    mod4 = lax.broadcasted_iota(jnp.int32, x.shape, 1) % 4
    up1, up2 = pltpu.roll(x, nr - 1, 1), pltpu.roll(x, nr - 2, 1)
    down1, down2 = pltpu.roll(x, 1, 1), pltpu.roll(x, 2, 1)
    above, inner, outer = mod4 >= 2, mod4 == 3, mod4 == 0
    slope = jnp.where(
        above,
        jnp.where(inner, 8.0 * up1, 0.0) - up2,
        down2 - jnp.where(outer, 8.0 * down1, 0.0),
    )
    curve = jnp.where(
        above,
        jnp.where(inner, 16.0 * up1, 0.0) - up2,
        jnp.where(outer, 16.0 * down1, 0.0) - down2,
    )
    return slope, curve


def temperature_kernel(
    vel, temp, base, s_near, s_far, a_far, a_near, r_left, r_right, cells, r_halo
):
    nt, na, nr = base.shape
    keep, rad, nrad = place()
    join_packs(r_halo, r_left, r_right, keep)
    inv12h, gt, lane = spacings(rad, nrad, nr)
    inv12, g = 1.0 / 12.0, VISCOSITY / 12.0
    turned = cells.reshape(na * nt, nr)
    s_even, a_even = is_even("sector"), is_even("ax")

    def s_low(f, k, out):
        return jnp.where(s_even, s_far[f, k, out], s_near[f, k, out])

    def s_high(f, k, out):
        return jnp.where(s_even, s_near[f, k, out], s_far[f, k, out])

    def a_low(f, k):
        return jnp.where(a_even, a_far[f, k], a_near[f, k])

    def a_high(f, k):
        return jnp.where(a_even, a_near[f, k], a_far[f, k])

    edge = (lane < 2) | (lane >= nr - 2)
    u_slope, _ = pack_parts(r_halo[1])
    t_slope, t_curve = pack_parts(r_halo[2])
    for t in range(nt):
        even, odd = (nr - 8 * t) % nr, (2 * nr - 8 * t - 4) % nr
        ts = pltpu.roll(t_slope, even, 1) if even else t_slope
        tc = pltpu.roll(t_curve, even, 1) if even else t_curve
        us = pltpu.roll(u_slope, odd, 1) if odd else u_slope
        for j in range(na // 8):
            out = slice(j * 8, j * 8 + 8)
            mid = temp[t, out]
            share = halo_share(mid, vel[2, t, out], inv12, g, (ts[out], tc[out]), (us[out],))
            value = base[t, out] + jnp.where(edge, share, 0.0)
            parts = None
            if t < 2:
                parts = [low_parts([s_low(f, k, out) for k in (0, 1)], t) for f in (4, 1)]
            elif t >= nt - 2:
                parts = [
                    high_parts([s_high(f, k, out) for k in (0, 1)], nt - 1 - t) for f in (4, 1)
                ]
            if parts is not None:
                value = value + halo_share(mid, vel[0, t, out], inv12h, gt, *parts)
            turned[pl.ds(j * 8 * nt + t, 8, stride=nt), :] = value
    rows, speeds = temp.reshape(nt * na, nr), vel.at[1].reshape(nt * na, nr)
    for a in (0, 1, na - 2, na - 1):
        mid, u = rows[pl.ds(a, nt, stride=na), :], speeds[pl.ds(a, nt, stride=na), :]
        if a < 2:
            parts = [low_parts([a_low(f, k) for k in (0, 1)], a) for f in (4, 2)]
            scale = keep[0]
        else:
            parts = [high_parts([a_high(f, k) for k in (0, 1)], na - 1 - a) for f in (4, 2)]
            scale = keep[1]
        cells[a] = cells[a] + scale * halo_share(mid, u, inv12, g, *parts)


def flow_kernel(
    rho, vel, temp, cells, s_near, s_far, a_far, a_near, r_left, r_right,
    new_rho, new_vel, new_temp,
    full, flux_t, flux_a, flux_r, press, r_halo,
):
    nt, na, nr = new_rho.shape
    keep, rad, nrad = place()
    for f, ref in enumerate((rho, vel.at[0], vel.at[1], vel.at[2], temp)):
        full[f, 2 : nt + 2, 8 : 8 + na] = ref[...]
    halos = (s_near, s_far, a_far, a_near, r_left, r_right)
    fill(full, halos, r_halo, keep)

    def products(t, carry):
        mass = 1.0 + full[0, t]
        flux_t[t] = mass * full[1, t]
        press[t] = mass * (1.0 + full[4, t])
        return carry

    lax.fori_loop(0, nt + 4, products, 0)

    def products_in(t, carry):
        mass = 1.0 + full[0, t + 2]
        flux_a[t + 2] = mass * full[2, t + 2]
        flux_r[t] = mass[8 : 8 + na] * full[3, t + 2, 8 : 8 + na]
        return carry

    lax.fori_loop(0, nt, products_in, 0)
    inv12h, gt, lane = spacings(rad, nrad, nr)
    inv12 = 1.0 / 12.0
    turned = cells.reshape(na * nt, nr)

    def step(t, carry):
        even, odd = (nr - 8 * t) % nr, (2 * nr - 8 * t - 4) % nr
        hr, h0, h1, h2, ht = [
            pltpu.roll(r_halo[f // 2], odd if f % 2 else even, 1) for f in range(5)
        ]
        turned_halo = [h0, h1, h2, (1.0 + hr) * h2, (1.0 + hr) * (1.0 + ht)]
        for j in range(na // 8):
            lo, out = 8 + j * 8, slice(j * 8, j * 8 + 8)
            halo = [x[out] for x in turned_halo]
            r0 = full[0, t + 2, lo : lo + 8]
            u = [full[1 + c, t + 2, lo : lo + 8] for c in range(3)]
            w = [u[0] * inv12h, u[1] * inv12, u[2] * inv12]
            scale = 1.0 / (HEAT_RATIO * (1.0 + r0))
            grads = [
                d1(t_shifts(press, t, lo)) * inv12h,
                d1(a_shifts(press, t, lo)) * inv12,
                d1(lane_shifts(press[t + 2, lo : lo + 8], halo[4], lane)) * inv12,
            ]
            for c in range(3):
                ref = full.at[1 + c]
                rate = transport(
                    u[c],
                    t_shifts(ref, t, lo),
                    a_shifts(ref, t, lo),
                    lane_shifts(u[c], halo[c], lane),
                    w,
                    gt,
                )
                new_vel[c, t, out] = u[c] + STEP_DT * (rate - grads[c] * scale)
            loss = (
                d1(t_shifts(flux_t, t, lo)) * inv12h
                + (
                    d1(a_shifts(flux_a, t, lo))
                    + d1(lane_shifts(flux_r[t, out], halo[3], lane))
                )
                * inv12
            )
            new_rho[t, out] = r0 - STEP_DT * loss
            new_temp[t, out] = turned[pl.ds(j * 8 * nt + t, 8, stride=nt), :]
        return carry

    lax.fori_loop(0, nt, step, 0)


def harmonics_kernel(table, spread, out):
    sectors, parts, nt, nr = spread.shape
    for p in range(parts):
        x = spread[:, p].reshape(sectors * nt, nr)
        y = jnp.dot(
            table[...], x, precision=lax.Precision.HIGHEST, preferred_element_type=jnp.float32
        )
        out[:, p] = y.reshape(sectors, HARM // sectors, nr)


def gather_kernel(parts, out):
    cells, rows, nr = parts.shape
    flat = parts.reshape(cells * rows, nr)
    for k in range(rows):
        out[k] = flat[pl.ds(k, cells, stride=rows), :]


def per_device(table, mass_excess, speed_vector, thermal_excess, energy_release):
    nt, na, nr = mass_excess.shape
    f32 = jnp.float32
    params = pltpu.CompilerParams(vmem_limit_bytes=VMEM_LIMIT)
    sds = jax.ShapeDtypeStruct
    hbm = pl.BlockSpec(memory_space=pltpu.HBM)
    vmem = pl.BlockSpec(memory_space=pltpu.VMEM)
    padded = (nt + 4, na + 16, nr)
    s_far, s_near = pl.pallas_call(
        sector_edges_kernel,
        in_specs=[hbm] * 3,
        out_specs=[vmem] * 2,
        out_shape=(sds((5, 2, na, nr), f32), sds((5, 2, na, nr), f32)),
        scratch_shapes=[pltpu.SemaphoreType.DMA((10,))],
        compiler_params=pltpu.CompilerParams(vmem_limit_bytes=54912 * 1024),
        name="sector_edges",
    )(mass_excess, speed_vector, thermal_excess)
    a_near, a_far, r_pack = pl.pallas_call(
        tile_edges_kernel,
        in_specs=[vmem] * 4,
        out_specs=[vmem] * 3,
        out_shape=(
            sds((5, 2, nt, nr), f32),
            sds((5, 2, nt, nr), f32),
            sds((PACK_PLANES, na, nr), f32),
        ),
        compiler_params=params,
        name="tile_edges",
    )(s_far, mass_excess, speed_vector, thermal_excess)

    def ring(axis, up):
        count = lax.axis_size(axis)
        return [(i, (i + (1 if up else -1)) % count) for i in range(count)]

    def pairs(axis, near):
        count = lax.axis_size(axis)
        return [(i, i ^ 1 if near else (i + (1 if i % 2 else -1)) % count) for i in range(count)]

    s_near = lax.ppermute(s_near, "sector", pairs("sector", True))
    s_far = lax.ppermute(s_far, "sector", pairs("sector", False))
    a_far = lax.ppermute(a_far, "ax", pairs("ax", False))
    a_near = lax.ppermute(a_near, "ax", pairs("ax", True))
    r_left = lax.ppermute(r_pack, "rad", ring("rad", True))
    r_right = lax.ppermute(r_pack, "rad", ring("rad", False))
    halos = (s_near, s_far, a_far, a_near, r_left, r_right)
    (base,) = pl.pallas_call(
        inner_kernel,
        in_specs=[vmem] * 3,
        out_specs=[vmem],
        out_shape=(sds((nt, na, nr), f32),),
        scratch_shapes=[pltpu.VMEM((3, *padded), f32)],
        cost_estimate=pl.CostEstimate(
            flops=80 * nt * na * nr, bytes_accessed=24 * nt * na * nr, transcendentals=0
        ),
        compiler_params=params,
        name="inner",
    )(speed_vector, thermal_excess, energy_release)
    (cells,) = pl.pallas_call(
        temperature_kernel,
        in_specs=[vmem] * 9,
        out_specs=[vmem],
        out_shape=(sds((na, nt, nr), f32),),
        scratch_shapes=[pltpu.VMEM((3, na, nr), f32)],
        compiler_params=params,
        name="temperature",
    )(speed_vector, thermal_excess, base, *halos)
    sectors = lax.axis_size("sector")
    rows = HARM // sectors
    share = na // sectors
    spread = lax.all_to_all(
        cells.reshape(sectors, share, nt, nr), "sector", 0, 0, tiled=True
    )
    new_rho, new_vel, new_temp = pl.pallas_call(
        flow_kernel,
        in_specs=[vmem] * 10,
        out_shape=(
            sds((nt, na, nr), f32),
            sds((3, nt, na, nr), f32),
            sds((nt, na, nr), f32),
        ),
        scratch_shapes=[
            pltpu.VMEM((5, *padded), f32),
            pltpu.VMEM(padded, f32),
            pltpu.VMEM(padded, f32),
            pltpu.VMEM((nt, na, nr), f32),
            pltpu.VMEM(padded, f32),
            pltpu.VMEM((3, na, nr), f32),
        ],
        cost_estimate=pl.CostEstimate(
            flops=180 * nt * na * nr, bytes_accessed=44 * nt * na * nr, transcendentals=0
        ),
        compiler_params=params,
        name="flow",
    )(mass_excess, speed_vector, thermal_excess, cells, *halos)
    spread, new_rho = lax.optimization_barrier((spread, new_rho))
    terms = pl.pallas_call(
        harmonics_kernel,
        in_specs=[vmem] * 2,
        out_specs=vmem,
        out_shape=sds((sectors, share, rows, nr), f32),
        compiler_params=params,
        name="harmonics",
    )(table, spread)
    terms = lax.all_to_all(terms, "sector", 0, 0, tiled=True)
    coeffs = pl.pallas_call(
        gather_kernel,
        out_shape=sds((rows, na, nr), f32),
        compiler_params=params,
        name="gather",
    )(terms.reshape(na, rows, nr))
    return (new_rho, new_vel, new_temp, coeffs)


def solution(mesh):
    cell = P("sector", "ax", "rad")
    vector = P(None, "sector", "ax", "rad")

    def run(mass_excess, speed_vector, thermal_excess, energy_release):
        table = jnp.asarray(basis_table(mass_excess.shape[0]))
        return jax.shard_map(
            per_device,
            mesh=mesh,
            in_specs=(P(), cell, vector, cell, cell),
            out_specs=(cell, vector, cell, cell),
            check_vma=False,
        )(table, mass_excess, speed_vector, thermal_excess, energy_release)

    return run
```
